128 devices in a mesh: frame: 16 (over y, x), height: 8 (over z, core).
Axes of the slice: x: 4, y: 4, z: 4, core: 2. Of those that a mesh axis runs over, the one named last changes fastest.
Arguments:
- tokens: bfloat16 [16, 106496], P(None, ('frame', 'height')), may hold values from -8 to 8
- token_pos: int32 [106496], P('frame'), may hold values from 0 to 106495, as said below
- weight_in: bfloat16 [3, 3, 3, 16, 512], replicated, may hold values from -0.3125 to 0.3125
- bias_in: float32 [512], replicated, may hold values from -1.8 to 1.8
- gain_one: float32 [512], replicated, may hold values from 0.1 to 1.9
- offset_one: float32 [512], replicated, may hold values from -3 to 3
- weight_one: bfloat16 [3, 3, 3, 512, 512], P(None, None, None, None, 'height'), may hold values from -0.0546875 to 0.0546875
- bias_one: float32 [512], replicated, may hold values from -1.8 to 1.8
- gain_two: float32 [512], replicated, may hold values from 0.1 to 1.9
- offset_two: float32 [512], replicated, may hold values from -3 to 3
- weight_two: bfloat16 [3, 3, 3, 512, 512], P(None, None, None, None, 'height'), may hold values from -0.0546875 to 0.0546875
- bias_two: float32 [512], replicated, may hold values from -1.8 to 1.8
- weight_time: bfloat16 [3, 512, 1024], replicated, may hold values from -0.15625 to 0.15625
- bias_time: float32 [1024], replicated, may hold values from -1.8 to 1.8
Outputs:
- frames_out: bfloat16 [64, 64, 208, 512], P('frame', 'height')
The draws below stay inside these ranges and needn't reach their ends.
Inputs may be any that keep to these rules, and one draw needn't show every extreme that they name: token_pos is a permutation of 0 .. 106495. The 832 entries of shard s = f * 8 + b (the shard's part of tokens along the frame+height split) are positions of frame slab f only (frames f * 2 .. f * 2 + 1), and hold exactly 104 positions of each height tile (rows g * 4 .. g * 4 + 3).
All inputs are finite; a program needn't handle non-finite values.
Results may differ from the reference program's by a relative error of at most 0.008.
Values may be sent and summed in bfloat16 or wider, within the bound.
No kernel may reach another device: no remote copies, remote signals or barrier semaphores. Data moves between devices by JAX's collectives and lax.ppermute only.
A program may use at most 192 MiB of HBM per device.

```python
import jax
import jax.numpy as jnp
from jax import lax

ZC = 16
CH = 512
GROUPS = 32
FT = 2
RH = 4
WD = 104
SLABS = 16
TILES = 8
TF = 32
HR = 32
TOK_DEV = 832
TOKENS = 106496


def ownership(key):
    keys = jax.random.split(key, 2 * SLABS * TILES)
    index = jnp.arange(TOK_DEV)
    within_frame = index // (RH * WD)
    within_row = index // WD % RH
    column = index % WD
    slab_ids = jnp.arange(SLABS)[:, None, None]
    tile_ids = jnp.arange(TILES)[None, :, None]
    places = ((slab_ids * FT + within_frame[None, None, :]) * HR + tile_ids * RH + within_row[None, None, :]) * WD + column[None, None, :]
    places = places.reshape(SLABS * TILES, TOK_DEV).astype(jnp.int32)
    mixed = jax.vmap(jax.random.permutation)(keys[:SLABS * TILES], places)
    share = TOK_DEV // TILES
    dealt = mixed.reshape(SLABS, TILES, TILES, share).transpose(0, 2, 1, 3).reshape(SLABS * TILES, TOK_DEV)
    final = jax.vmap(jax.random.permutation)(keys[SLABS * TILES:], dealt)
    return final.reshape(-1).astype(jnp.int32)


def draw_token_pos(key, part):
    return ownership(key)


def scene_field(key, places):
    frame_of = places // (HR * WD)
    row_of = places // WD % HR
    frame_pos = frame_of.astype(jnp.float32)
    row_pos = row_of.astype(jnp.float32)
    parts = jax.random.split(key, 5)
    row_amp = jax.random.uniform(parts[0], (ZC, 1), jnp.float32, -1.5, 1.5)
    row_phase = jax.random.uniform(parts[1], (ZC, 1), jnp.float32, -3.14159, 3.14159)
    frame_amp = jax.random.uniform(parts[2], (ZC, 1), jnp.float32, -1.5, 1.5)
    frame_phase = jax.random.uniform(parts[3], (ZC, 1), jnp.float32, -3.14159, 3.14159)
    region_table = jax.random.uniform(parts[4], (ZC, SLABS * TILES), jnp.float32, -1.0, 1.0)
    region = frame_of // FT * TILES + row_of // RH
    rough = jnp.take(region_table, region, axis=1)
    smooth_rows = row_amp * jnp.cos(3.14159 * (row_pos[None, :] + 0.5) / HR + row_phase)
    smooth_frames = frame_amp * jnp.cos(3.14159 * (frame_pos[None, :] + 0.5) / TF + frame_phase)
    return smooth_rows + smooth_frames + rough


def draw_tokens(key, part):
    places = ownership(key)
    key = jax.random.fold_in(key, 11)
    frame_of = (places // (HR * WD)).astype(jnp.float32)
    level = 0.6 * jnp.power(3.0, frame_of / max(TF - 1, 1))
    scene = scene_field(jax.random.fold_in(key, 7), places)
    values = jnp.clip(jax.random.normal(key, (ZC, TOKENS), jnp.float32) * level[None, :] + scene, -8.0, 8.0)
    return values.astype(jnp.bfloat16)


def steps_of(key, shape, cuts, smallest, high):
    def one(dim, blocks):
        steps = jax.random.uniform(jax.random.fold_in(jax.random.fold_in(key, 6), dim), (blocks,), jnp.float32, smallest / len(cuts), high / len(cuts))
        return jnp.repeat(jnp.exp(steps), shape[dim] // blocks).reshape((-1,) + (1,) * (len(shape) - dim - 1))

    factor_of = one(*cuts[0])
    for cut in cuts[1:]:
        factor_of = factor_of * one(*cut)
    return factor_of


def centred(rng, dims, width, most, cuts=(), kind=jnp.bfloat16):
    entries = jax.random.normal(rng, dims, jnp.float32) * width
    if len(cuts) > 0:
        entries = steps_of(rng, dims, cuts, -0.22, 0.18) * entries
    return jnp.clip(entries, min=-most, max=most).astype(kind)


def setup_inputs(seed: int = 0) -> dict:
    splits = jax.random.split(jax.random.key(seed), 15)
    return {
        "tokens": draw_tokens(jax.random.fold_in(splits[14], 71), 0),
        "token_pos": draw_token_pos(jax.random.fold_in(splits[14], 71), 0),
        "weight_in": centred(splits[2], (3, 3, 3, ZC, CH), (27 * ZC) ** -0.5, 0.3125),
        "bias_in": centred(splits[3], (CH,), 0.3, 1.8, (), jnp.float32),
        "gain_one": jnp.clip(1.0 + 0.18 * jax.random.normal(splits[4], (CH,), jnp.float32), 0.1, 1.9),
        "offset_one": centred(splits[5], (CH,), 0.5, 3.0, (), jnp.float32),
        "weight_one": centred(splits[6], (3, 3, 3, CH, CH), (27 * CH) ** -0.5, 0.0546875, ((4, 8),)),
        "bias_one": centred(splits[7], (CH,), 0.3, 1.8, (), jnp.float32),
        "gain_two": jnp.clip(1.0 + 0.18 * jax.random.normal(splits[8], (CH,), jnp.float32), 0.1, 1.9),
        "offset_two": centred(splits[9], (CH,), 0.5, 3.0, (), jnp.float32),
        "weight_two": centred(splits[10], (3, 3, 3, CH, CH), (27 * CH) ** -0.5, 0.0546875, ((4, 8),)),
        "bias_two": centred(splits[11], (CH,), 0.3, 1.8, (), jnp.float32),
        "weight_time": centred(splits[12], (3, CH, 2 * CH), (3 * CH) ** -0.5, 0.15625),
        "bias_time": centred(splits[13], (2 * CH,), 0.3, 1.8, (), jnp.float32),
    }


def causal_conv(field, kernel):
    frames, rows, cells, inner = field.shape
    padded = jnp.pad(field, ((2, 0), (1, 1), (1, 1), (0, 0)))
    total = jnp.zeros((frames * rows * cells, kernel.shape[-1]), jnp.float32)
    for lag in range(3):
        for rise in range(3):
            for across in range(3):
                piece = padded[lag:lag + frames, rise:rise + rows, across:across + cells].reshape(-1, inner)
                total = total + jnp.dot(piece, kernel[lag, rise, across], preferred_element_type=jnp.float32)
    return total

def group_norm(values, gain, offset):
    count = values.shape[0]
    grouped = values.astype(jnp.float32).reshape(count, GROUPS, CH // GROUPS)
    mean = lax.optimization_barrier(jnp.mean(grouped, axis=(0, 2)))
    centered = grouped - mean[None, :, None]
    variance = lax.optimization_barrier(jnp.mean(centered * centered, axis=(0, 2)))
    normed = centered * lax.rsqrt(variance + 1e-06)[None, :, None]
    return normed.reshape(count, CH) * gain + offset

def reference(tokens, token_pos, weight_in, bias_in, gain_one, offset_one, weight_one, bias_one, gain_two, offset_two, weight_two, bias_two, weight_time, bias_time):
    flat = jnp.zeros((ZC, TF * HR * WD), tokens.dtype).at[:, token_pos].set(tokens)
    latent = flat.reshape(ZC, TF, HR, WD).transpose(1, 2, 3, 0)
    base = (causal_conv(latent, weight_in) + bias_in).astype(jnp.bfloat16)
    first = jax.nn.silu(group_norm(base, gain_one, offset_one)).astype(jnp.bfloat16)
    inner = (causal_conv(first.reshape(TF, HR, WD, CH), weight_one) + bias_one).astype(jnp.bfloat16)
    second = jax.nn.silu(group_norm(inner, gain_two, offset_two)).astype(jnp.bfloat16)
    block = (base.astype(jnp.float32) + causal_conv(second.reshape(TF, HR, WD, CH), weight_two) + bias_two).astype(jnp.bfloat16)
    block = block.reshape(TF, HR, WD, CH)
    padded = jnp.pad(block, ((2, 0), (0, 0), (0, 0), (0, 0)))
    total = jnp.zeros((TF * HR * WD, 2 * CH), jnp.float32)
    for lag in range(3):
        total = total + jnp.dot(padded[lag:lag + TF].reshape(-1, CH), weight_time[lag], preferred_element_type=jnp.float32)
    doubled = (total + bias_time).astype(jnp.bfloat16)
    doubled = doubled.reshape(TF, HR, WD, 2, CH).transpose(0, 3, 1, 2, 4).reshape(2 * TF, HR, WD, CH)
    return jnp.repeat(jnp.repeat(doubled, 2, axis=1), 2, axis=2)
```

```python
import functools

import jax
import jax.numpy as jnp
from jax import lax
from jax.experimental import pallas as pl
from jax.experimental.pallas import tpu as pltpu
from jax.sharding import PartitionSpec as P

GROUPS = 32
FT = 2
RH = 4
WD = 104
WP = 112
CH = 512
CELLS = FT * RH * WD
F32 = jnp.float32
BF16 = jnp.bfloat16
NT = (((1,), (1,)), ((), ()))
TN = (((0,), (0,)), ((), ()))
VMEM = pl.BlockSpec(memory_space=pltpu.VMEM)
SMEM = pl.BlockSpec(memory_space=pltpu.SMEM)
ANY = pl.BlockSpec(memory_space=pl.ANY)
EXACT = lax.Precision.HIGHEST
LIMIT = 56 * 2**20


def along(value, axis, steps):
    count = lax.axis_size(axis)
    leading, last = (max(0, -steps), min(count, count - steps))
    return lax.ppermute(value, axis, [(source, source + steps) for source in range(leading, last)])


def spread(rows, cols, lanes_first, shift):
    one = lax.broadcasted_iota(jnp.int32, (rows, cols), 0)
    two = lax.broadcasted_iota(jnp.int32, (rows, cols), 1)
    lane, channel = (one, two) if lanes_first else (two, one)
    return (lane == channel // (CH // GROUPS) + shift).astype(F32)


def local_stats(values, stat_ref):
    cells = values.shape[0]
    total = jnp.broadcast_to(jnp.sum(values, axis=0, keepdims=True), (8, CH))
    size = cells * (CH // GROUPS)
    mean = jnp.dot(total, spread(CH, 128, False, 0), precision=EXACT, preferred_element_type=F32) / size
    per_channel = jnp.dot(mean, spread(128, CH, True, 0), precision=EXACT, preferred_element_type=F32)
    centered = values - per_channel[:1]
    square = jnp.broadcast_to(jnp.sum(centered * centered, axis=0, keepdims=True), (8, CH))
    spread_sq = jnp.dot(square, spread(CH, 128, False, GROUPS), precision=EXACT, preferred_element_type=F32)
    stat_ref[...] = jnp.broadcast_to((mean + spread_sq)[:1], stat_ref.shape)


def combine_stats(stats_ref, size):
    stats = stats_ref[...]
    devices = stats.shape[0]
    means = jnp.dot(stats, spread(128, CH, True, 0), precision=EXACT, preferred_element_type=F32)
    squares = jnp.dot(stats, spread(128, CH, True, GROUPS), precision=EXACT, preferred_element_type=F32)
    mean = jnp.sum(means, axis=0, keepdims=True) / devices
    away = means - mean
    total = jnp.sum(squares + size * (away * away), axis=0, keepdims=True)
    return mean, lax.rsqrt(total / (size * devices) + 1e-06)


def share_stats(stat):
    return lax.all_to_all(stat, ("frame", "height"), 0, 0, tiled=True)


def input_kernel(lat_ref, w_ref, bias_ref, base_ref, stat_ref):
    w = w_ref[...]
    for t in range(2 * FT):
        columns = []
        for r in range(RH + 2):
            columns.append(jnp.concatenate([lat_ref[t + a, r + b] for a in range(3) for b in range(3)], axis=0))
        field = jnp.concatenate(columns, axis=1)
        total = lax.dot_general(field, w, TN, preferred_element_type=F32)
        total = (total + bias_ref[...]).astype(BF16).reshape(RH + 2, 128, CH)
        base_ref[t] = total[:, :WD]
    own = base_ref[FT:, 1 : RH + 1].reshape(CELLS, CH).astype(F32)
    local_stats(own, stat_ref)


def input_conv(latent, weight, bias, devices):
    return pl.pallas_call(
        input_kernel,
        in_specs=[VMEM, VMEM, VMEM],
        out_specs=[VMEM, VMEM],
        out_shape=[
            jax.ShapeDtypeStruct((2 * FT, RH + 2, WD, CH), BF16),
            jax.ShapeDtypeStruct((devices, 128), F32),
        ],
        compiler_params=pltpu.CompilerParams(vmem_limit_bytes=LIMIT),
        cost_estimate=pl.CostEstimate(flops=3 * 10**9, bytes_accessed=4 * 10**6, transcendentals=0),
        name="input_conv",
    )(latent, weight, bias)


def conv_kernel(pieces, products, taps, extras, *refs):
    refs = list(refs)
    raws = [refs.pop(0) for _ in pieces]
    stats_ref, flags_ref, gain_ref, offset_ref, w_ref = [refs.pop(0) for _ in range(5)]
    partial_ref = refs.pop(0) if "partial" in extras else None
    bias_ref = refs.pop(0) if "bias" in extras else None
    base_ref = refs.pop(0) if "base" in extras else None
    out_ref = refs.pop(0)
    stat_ref = refs.pop(0) if "stat" in extras else None
    field, wbuf, acc, sems = refs
    copies = [
        pltpu.make_async_copy(w_ref.at[pl.ds(taps[0], len(taps)), :, e], wbuf.at[e], sems.at[e]) for e in range(3)
    ]
    for copy in copies:
        copy.start()
    mean, inverse = combine_stats(stats_ref, CELLS * (CH // GROUPS))
    scale = inverse * gain_ref[...]
    offset = offset_ref[...]
    for raw, (frame, frames, row, rows, flag_of) in zip(raws, pieces):
        for i in range(frames):
            for j in range(rows):
                value = (raw[i, j].astype(F32) - mean) * scale + offset
                half = 0.5 * value
                value = half + half * jnp.tanh(half)
                for which in flag_of(i, j):
                    value = value * flags_ref[which]
                field[frame + i, row + j, :WD] = value.astype(BF16)
                field[frame + i, row + j, WD:] = jnp.zeros((WP - WD, CH), BF16)
    for e in range(3):
        copies[e].wait()
        for t in range(FT):
            terms = [(f, a) for (out, f, a) in products if out == t]
            xs = [field[f, b : b + RH].reshape(RH * WP, CH) for f, a in terms for b in range(3)]
            ws = [wbuf[e, a - taps[0], b] for f, a in terms for b in range(3)]
            acc[e, pl.ds(t * RH * WP, RH * WP)] = lax.dot_general(
                jnp.concatenate(xs, axis=1), jnp.concatenate(ws, axis=1), NT, preferred_element_type=F32
            )
    edge = jnp.zeros((1, CH), F32)
    total = acc[1] + jnp.concatenate([edge, acc[0, :-1]], axis=0) + jnp.concatenate([acc[2, 1:], edge], axis=0)
    total = total.reshape(FT, RH, WP, CH)[:, :, :WD]
    if partial_ref is not None:
        total = total + partial_ref[...]
    if bias_ref is not None:
        total = total + bias_ref[...]
    if base_ref is not None:
        total = total + base_ref[FT:, 1 : RH + 1].astype(F32)
    out_ref[...] = total.astype(out_ref.dtype)
    if stat_ref is not None:
        local_stats(total.astype(BF16).astype(F32).reshape(CELLS, CH), stat_ref)


def block_conv(name, raws, pieces, products, stats, flags, gain, offset, weight, extras, kind, devices):
    taps = sorted({a for _, _, a in products})
    frames = max(f for _, f, _ in products) + 1
    args = [*raws, stats, flags, gain, offset, weight, *[extras[k] for k in ("partial", "bias", "base") if k in extras]]
    specs = [*[VMEM] * len(raws), VMEM, SMEM, VMEM, VMEM, ANY]
    specs += [VMEM] * (len(args) - len(specs))
    shapes = [jax.ShapeDtypeStruct((FT, RH, WD, CH), kind)]
    if "stat" in extras:
        shapes.append(jax.ShapeDtypeStruct((devices, 128), F32))
    return pl.pallas_call(
        functools.partial(conv_kernel, pieces, products, taps, tuple(extras)),
        in_specs=specs,
        out_specs=[VMEM] * len(shapes),
        out_shape=shapes,
        scratch_shapes=[
            pltpu.VMEM((frames, RH + 2, WP, CH), BF16),
            pltpu.VMEM((3, len(taps), 3, CH, CH), BF16),
            pltpu.VMEM((3, FT * RH * WP, CH), F32),
            pltpu.SemaphoreType.DMA((3,)),
        ],
        compiler_params=pltpu.CompilerParams(vmem_limit_bytes=LIMIT),
        cost_estimate=pl.CostEstimate(
            flops=len(products) * 2 * 9 * RH * WP * CH * CH, bytes_accessed=16 * 10**6, transcendentals=0
        ),
        name=name,
    )(*args)


def upsample_kernel(halo_ref, block_ref, w_ref, bias_ref, out_ref):
    t = pl.program_id(0)
    s = pl.program_id(1)
    cells = RH * WD
    halo = [halo_ref[i].reshape(cells, CH) for i in range(FT)]
    own = [block_ref[i].reshape(cells, CH) for i in range(FT)]

    def emit(parts):
        field = jnp.concatenate(parts, axis=1)
        w = w_ref[...].reshape(3 * CH, CH)
        total = jnp.dot(field, w, preferred_element_type=F32) + bias_ref[...]
        total = total.astype(BF16).astype(F32).reshape(RH, WD, CH)
        for r in range(RH):
            wide = jnp.broadcast_to(total[r][:, None, :], (WD, 2, CH)).reshape(2 * WD, CH).astype(BF16)
            out_ref[0, 2 * r] = wide
            out_ref[0, 2 * r + 1] = wide

    @pl.when(t == 0)
    def _():
        emit([halo[0], halo[1], own[0]])

    @pl.when(t == 1)
    def _():
        emit([halo[1], own[0], own[1]])


def upsample(halo, block, weight, bias):
    return pl.pallas_call(
        upsample_kernel,
        grid=(FT, 2),
        in_specs=[
            pl.BlockSpec((FT, RH, WD, CH), lambda t, s: (0, 0, 0, 0)),
            pl.BlockSpec((FT, RH, WD, CH), lambda t, s: (0, 0, 0, 0)),
            pl.BlockSpec((3, CH, CH), lambda t, s: (0, 0, s)),
            pl.BlockSpec((1, CH), lambda t, s: (0, s)),
        ],
        out_specs=pl.BlockSpec((1, 2 * RH, 2 * WD, CH), lambda t, s: (2 * t + s, 0, 0, 0)),
        out_shape=jax.ShapeDtypeStruct((2 * FT, 2 * RH, 2 * WD, CH), BF16),
        compiler_params=pltpu.CompilerParams(vmem_limit_bytes=LIMIT),
        cost_estimate=pl.CostEstimate(flops=3 * 10**9, bytes_accessed=12 * 10**6, transcendentals=0),
        name="upsample",
    )(halo, block, weight, bias)


def own_latent(tokens, token_pos):
    tiles = lax.axis_size("height")
    mine = lax.axis_index("height")
    slab = lax.axis_index("frame")
    local_count = tokens.shape[1]
    share = local_count // tiles
    total_rows = RH * tiles
    table = token_pos.reshape(tiles, local_count)
    frame_in = table // (total_rows * WD) - slab * FT
    row_all = table // WD % total_rows
    tile_of = row_all // RH
    local_index = (frame_in * RH + row_all % RH) * WD + table % WD
    sort_keys = tile_of * local_count + local_index
    own_keys = lax.dynamic_index_in_dim(sort_keys, mine, 0, keepdims=False)
    outgoing = jnp.take(tokens, jnp.argsort(own_keys), axis=1)
    incoming = lax.all_to_all(outgoing, "height", split_axis=1, concat_axis=1, tiled=True)
    ordered = jnp.sort(sort_keys, axis=1)
    arriving = lax.dynamic_slice_in_dim(ordered, mine * share, share, 1)
    targets = (arriving % local_count).reshape(-1)
    grid = jnp.zeros((tokens.shape[0], local_count), tokens.dtype).at[:, targets].set(incoming)
    return grid.reshape(tokens.shape[0], FT, RH, WD).transpose(1, 2, 0, 3)


def latent_field(latent):
    above = along(latent[:, RH - 2 :], "height", 1)
    below = along(latent[:, :2], "height", -1)
    taller = jnp.concatenate([above, latent, below], axis=1)
    field = jnp.concatenate([along(taller, "frame", 2), along(taller, "frame", 1), taller], axis=0)
    padded = jnp.pad(field, ((0, 0), (0, 0), (0, 0), (1, 129 - WD)))
    return jnp.concatenate([padded[..., e : e + 128] for e in range(3)], axis=2)


def on_device(
    tokens,
    token_pos,
    weight_in,
    bias_in,
    gain_one,
    offset_one,
    weight_one,
    bias_one,
    gain_two,
    offset_two,
    weight_two,
    bias_two,
    weight_time,
    bias_time,
):
    devices = lax.axis_size("frame") * lax.axis_size("height")
    kernel_one = lax.all_gather(jnp.swapaxes(weight_one, 3, 4), "height", axis=3, tiled=True)
    kernel_two = lax.all_gather(jnp.swapaxes(weight_two, 3, 4), "height", axis=3, tiled=True)
    slab, tile = lax.axis_index("frame"), lax.axis_index("height")
    flags = jnp.stack([slab > 0, tile > 0, tile < lax.axis_size("height") - 1]).astype(F32)
    row = lambda v: v.reshape(1, -1)

    latent = latent_field(own_latent(tokens, token_pos))
    base, stat = input_conv(latent, weight_in.reshape(-1, CH), row(bias_in), devices)

    def edges(j):
        return [1] if j == 0 else [2] if j == RH + 1 else []

    everything = lambda i, j: ([0] if i < FT else []) + edges(j)
    inner, stat = block_conv(
        "conv_one",
        [base],
        [(0, 2 * FT, 0, RH + 2, everything)],
        [(t, t + a, a) for t in range(FT) for a in range(3)],
        share_stats(stat),
        flags,
        row(gain_one),
        row(offset_one),
        kernel_one,
        {"bias": row(bias_one), "stat": None},
        BF16,
        devices,
    )
    behind = along(inner, "frame", 1)
    shared = share_stats(stat)

    def rows_around(v):
        return [along(v[:, RH - 1 :], "height", 1), v, along(v[:, :1], "height", -1)]

    pieces = lambda more: [
        (0, FT, 0, 1, lambda i, j: more + [1]),
        (0, FT, 1, RH, lambda i, j: more),
        (0, FT, RH + 1, 1, lambda i, j: more + [2]),
    ]
    (partial,) = block_conv(
        "conv_two_own",
        rows_around(inner),
        pieces([]),
        [(0, 0, 2), (1, 0, 1), (1, 1, 2)],
        shared,
        flags,
        row(gain_two),
        row(offset_two),
        kernel_two,
        {},
        F32,
        devices,
    )
    (block,) = block_conv(
        "conv_two_behind",
        rows_around(behind),
        pieces([0]),
        [(0, 0, 0), (0, 1, 1), (1, 1, 0)],
        shared,
        flags,
        row(gain_two),
        row(offset_two),
        kernel_two,
        {"partial": partial, "bias": row(bias_two), "base": base},
        BF16,
        devices,
    )
    return upsample(along(block, "frame", 1), block, weight_time, row(bias_time))


def solution(mesh):
    placed = (
        P(None, ("frame", "height")),
        P("frame"),
        P(),
        P(),
        P(),
        P(),
        P(None, None, None, None, "height"),
        P(),
        P(),
        P(),
        P(None, None, None, None, "height"),
        P(),
        P(),
        P(),
    )
    return jax.shard_map(
        on_device,
        mesh=mesh,
        in_specs=placed,
        out_specs=P("frame", "height", None, None),
        check_vma=False,
    )
```

```python
import functools

import jax
import jax.numpy as jnp
from jax import lax
from jax.experimental import pallas as pl
from jax.experimental.pallas import tpu as pltpu
from jax.sharding import PartitionSpec as P

GROUPS = 32
ZC = 16
FT = 2
RH = 4
WD = 104
WP = 112
CH = 512
CELLS = FT * RH * WD
F32 = jnp.float32
BF16 = jnp.bfloat16
NT = (((1,), (1,)), ((), ()))
TN = (((0,), (0,)), ((), ()))
VMEM = pl.BlockSpec(memory_space=pltpu.VMEM)
SMEM = pl.BlockSpec(memory_space=pltpu.SMEM)
ANY = pl.BlockSpec(memory_space=pl.ANY)
EXACT = lax.Precision.HIGHEST
LIMIT = 56 * 2**20


def along(value, axis, steps):
    count = lax.axis_size(axis)
    leading, last = (max(0, -steps), min(count, count - steps))
    return lax.ppermute(value, axis, [(source, source + steps) for source in range(leading, last)])


def spread(rows, cols, lanes_first, shift):
    one = lax.broadcasted_iota(jnp.int32, (rows, cols), 0)
    two = lax.broadcasted_iota(jnp.int32, (rows, cols), 1)
    lane, channel = (one, two) if lanes_first else (two, one)
    return (lane == channel // (CH // GROUPS) + shift).astype(F32)


def local_stats(values, stat_ref):
    cells = values.shape[0]
    total = jnp.broadcast_to(jnp.sum(values, axis=0, keepdims=True), (8, CH))
    size = cells * (CH // GROUPS)
    mean = jnp.dot(total, spread(CH, 128, False, 0), precision=EXACT, preferred_element_type=F32) / size
    per_channel = jnp.dot(mean, spread(128, CH, True, 0), precision=EXACT, preferred_element_type=F32)
    centered = values - per_channel[:1]
    square = jnp.broadcast_to(jnp.sum(centered * centered, axis=0, keepdims=True), (8, CH))
    spread_sq = jnp.dot(square, spread(CH, 128, False, GROUPS), precision=EXACT, preferred_element_type=F32)
    stat_ref[...] = jnp.broadcast_to((mean + spread_sq)[:1], stat_ref.shape)


def combine_stats(stats_ref, size):
    stats = stats_ref[...]
    devices = stats.shape[0]
    means = jnp.dot(stats, spread(128, CH, True, 0), precision=EXACT, preferred_element_type=F32)
    squares = jnp.dot(stats, spread(128, CH, True, GROUPS), precision=EXACT, preferred_element_type=F32)
    mean = jnp.sum(means, axis=0, keepdims=True) / devices
    away = means - mean
    total = jnp.sum(squares + size * (away * away), axis=0, keepdims=True)
    return mean, lax.rsqrt(total / (size * devices) + 1e-06)


def share_stats(stat):
    return lax.all_to_all(stat, ("frame", "height"), 0, 0, tiled=True)


def input_kernel(early_ref, behind_ref, own_ref, w_ref, bias_ref, base_ref, stat_ref):
    w = w_ref[...]
    lat = {}
    for k, ref in enumerate((early_ref, behind_ref, own_ref)):
        for i in range(FT):
            for r in range(RH + 4):
                value = ref[i, r].astype(F32)
                shifts = [value] + [pltpu.roll(value, 128 - e, 1) for e in (1, 2)]
                lat[k * FT + i, r] = jnp.concatenate([v.astype(BF16) for v in shifts], axis=0)
    for t in range(2 * FT):
        columns = []
        for r in range(RH + 2):
            columns.append(jnp.concatenate([lat[t + a, r + b] for a in range(3) for b in range(3)], axis=0))
        field = jnp.concatenate(columns, axis=1)
        total = lax.dot_general(field, w, TN, preferred_element_type=F32)
        total = (total + bias_ref[...]).astype(BF16).reshape(RH + 2, 128, CH)
        base_ref[t] = total[:, :WD]
    own = base_ref[FT:, 1 : RH + 1].reshape(CELLS, CH).astype(F32)
    local_stats(own, stat_ref)


def input_conv(latent, weight, bias, devices):
    return pl.pallas_call(
        input_kernel,
        in_specs=[VMEM] * 5,
        out_specs=[VMEM, VMEM],
        out_shape=[
            jax.ShapeDtypeStruct((2 * FT, RH + 2, WD, CH), BF16),
            jax.ShapeDtypeStruct((devices, 128), F32),
        ],
        compiler_params=pltpu.CompilerParams(vmem_limit_bytes=LIMIT),
        cost_estimate=pl.CostEstimate(flops=3 * 10**9, bytes_accessed=4 * 10**6, transcendentals=0),
        name="input_conv",
    )(*latent, weight, bias)


def ring_gather(unit, send, pos):
    units = unit.shape[0]
    quarter = lax.dynamic_slice_in_dim(unit, pos * 16, 16, axis=2)
    tiles = lax.axis_size("height")
    over = lambda k: [(i, (i + 2 * k) % tiles) for i in range(tiles)]
    piece = jnp.concatenate([lax.ppermute(quarter, "height", over(k)) for k in (1, 3, 2)], axis=0)
    half = (piece.shape[0] + 1) // 2
    left, right = send(piece, 1), send(piece, -1)
    left2, right2 = send(left[:half], 1), send(right[half:], -1)
    quarters = [unit[:, :, 16 * k : 16 * k + 16] for k in range(4)]
    held = jnp.concatenate([piece, left, right, left2, right2, *quarters], axis=0)
    other = lax.ppermute(held, "height", [(i, i ^ 1) for i in range(tiles)])
    return [piece, left, right, left2, right2, unit, other], units, half


def ring_plan(arrays, units, half, columns, axis, first):
    plan = []
    full = 3 * units

    def add(array, start, low, high, flip, place):
        index = low
        while index < high:
            stop = min(high, index - index % 3 + 3)
            shift, e, a = index // units, index % units // 3, index % 3
            z = 0 if place == "own" else (3, 1, 2)[shift]
            plan.append((array, start + index - low, stop - index, columns[e], a, 16, (flip, z, axis, place)))
            index = stop

    for flip in (0, 1):
        base = 0
        for k, (low, high, ring) in enumerate([(0, full, 0), (0, full, 3), (0, full, 1), (0, half, 2), (half, full, 2)]):
            add(first + (6 if flip else k), base if flip else 0, low, high, flip, ring)
            base += high - low
        for q in range(4 if flip else 1):
            for u in range(units // 3):
                start = (base + q * units if flip else 0) + 3 * u
                rows = 16 if flip else 64
                plan.append((first + (6 if flip else 5), start, 3, columns[u], 0, rows, (flip, 0, None, q)))
    return arrays, plan


def conv_kernel(pieces, products, taps, plan, weights, extras, *refs):
    refs = list(refs)
    raws = [refs.pop(0) for _ in pieces]
    stats_ref, flags_ref, place_ref, gain_ref, offset_ref = [refs.pop(0) for _ in range(5)]
    w_refs = [refs.pop(0) for _ in range(weights)]
    partial_ref = refs.pop(0) if "partial" in extras else None
    bias_ref = refs.pop(0) if "bias" in extras else None
    base_ref = refs.pop(0) if "base" in extras else None
    out_ref = refs.pop(0)
    stat_ref = refs.pop(0) if "stat" in extras else None
    field, wbuf, acc, sems = refs
    low, high = taps[0], taps[-1] + 1
    z, core = place_ref[0], place_ref[1]
    for e in range(3):
        for array, start, length, column, a, rows, where in plan:
            if column != e:
                continue
            begin, end = max(a, low), min(a + length, high)
            if begin >= end:
                continue
            if where is None:
                source = w_refs[array].at[pl.ds(begin, end - begin), :, start]
                target = wbuf.at[e, pl.ds(begin - low, end - begin)]
            else:
                flip, shift, ring, step = where
                block = lax.rem(z + shift, 4) * 2 + (1 - core if flip else core)
                quarter = step if ring is None else lax.rem(place_ref[ring] + step, 4)
                offset = pl.multiple_of(block * 64 + quarter * 16, 16)
                source = w_refs[array].at[pl.ds(start + begin - a, end - begin)]
                target = wbuf.at[e, pl.ds(begin - low, end - begin), :, pl.ds(offset, rows)]
            pltpu.make_async_copy(source, target, sems.at[e]).start()
    mean, inverse = combine_stats(stats_ref, CELLS * (CH // GROUPS))
    scale = inverse * gain_ref[...]
    offset = offset_ref[...]
    for raw, (frame, frames, row, rows, flag_of) in zip(raws, pieces):
        for i in range(frames):
            for j in range(rows):
                value = (raw[i, j].astype(F32) - mean) * scale + offset
                half = 0.5 * value
                value = half + half * jnp.tanh(half)
                for which in flag_of(i, j):
                    value = value * flags_ref[which]
                field[frame + i, row + j, :WD] = value.astype(BF16)
                field[frame + i, row + j, WD:] = jnp.zeros((WP - WD, CH), BF16)
    for e in range(3):
        pltpu.make_async_copy(wbuf.at[e], wbuf.at[e], sems.at[e]).wait()
        for t in range(FT):
            terms = [(f, a) for (out, f, a) in products if out == t]
            xs = [field[f, b : b + RH].reshape(RH * WP, CH) for f, a in terms for b in range(3)]
            ws = [wbuf[e, a - low, b] for f, a in terms for b in range(3)]
            acc[e, pl.ds(t * RH * WP, RH * WP)] = lax.dot_general(
                jnp.concatenate(xs, axis=1), jnp.concatenate(ws, axis=1), NT, preferred_element_type=F32
            )
    edge = jnp.zeros((1, CH), F32)
    total = acc[1] + jnp.concatenate([edge, acc[0, :-1]], axis=0) + jnp.concatenate([acc[2, 1:], edge], axis=0)
    total = total.reshape(FT, RH, WP, CH)[:, :, :WD]
    if partial_ref is not None:
        total = total + partial_ref[...]
    if bias_ref is not None:
        total = total + bias_ref[...]
    if base_ref is not None:
        total = total + base_ref[FT:, 1 : RH + 1].astype(F32)
    out_ref[...] = total.astype(out_ref.dtype)
    if stat_ref is not None:
        local_stats(total.astype(BF16).astype(F32).reshape(CELLS, CH), stat_ref)


def block_conv(name, raws, pieces, products, stats, flags, place, gain, offset, weight, extras, kind, devices):
    arrays, plan = weight
    taps = sorted({a for _, _, a in products})
    frames = max(f for _, f, _ in products) + 1
    args = [*raws, stats, flags, place, gain, offset, *arrays]
    args += [extras[k] for k in ("partial", "bias", "base") if k in extras]
    specs = [*[VMEM] * len(raws), VMEM, SMEM, SMEM, VMEM, VMEM, *[ANY] * len(arrays)]
    specs += [VMEM] * (len(args) - len(specs))
    shapes = [jax.ShapeDtypeStruct((FT, RH, WD, CH), kind)]
    if "stat" in extras:
        shapes.append(jax.ShapeDtypeStruct((devices, 128), F32))
    return pl.pallas_call(
        functools.partial(conv_kernel, pieces, products, taps, plan, len(arrays), tuple(extras)),
        in_specs=specs,
        out_specs=[VMEM] * len(shapes),
        out_shape=shapes,
        scratch_shapes=[
            pltpu.VMEM((frames, RH + 2, WP, CH), BF16),
            pltpu.VMEM((3, len(taps), 3, CH, CH), BF16),
            pltpu.VMEM((3, FT * RH * WP, CH), F32),
            pltpu.SemaphoreType.DMA((3,)),
        ],
        compiler_params=pltpu.CompilerParams(vmem_limit_bytes=LIMIT),
        cost_estimate=pl.CostEstimate(
            flops=len(products) * 2 * 9 * RH * WP * CH * CH, bytes_accessed=16 * 10**6, transcendentals=0
        ),
        name=name,
    )(*args)


def upsample_kernel(halo_ref, block_ref, w_ref, bias_ref, out_ref):
    t = pl.program_id(0)
    s = pl.program_id(1)
    cells = RH * WD
    halo = [halo_ref[i].reshape(cells, CH) for i in range(FT)]
    own = [block_ref[i].reshape(cells, CH) for i in range(FT)]

    def emit(parts):
        field = jnp.concatenate(parts, axis=1)
        w = w_ref[...].reshape(3 * CH, CH)
        total = jnp.dot(field, w, preferred_element_type=F32) + bias_ref[...]
        total = total.astype(BF16).astype(F32).reshape(RH, WD, CH)
        for r in range(RH):
            wide = jnp.broadcast_to(total[r][:, None, :], (WD, 2, CH)).reshape(2 * WD, CH).astype(BF16)
            out_ref[0, 2 * r] = wide
            out_ref[0, 2 * r + 1] = wide

    @pl.when(t == 0)
    def _():
        emit([halo[0], halo[1], own[0]])

    @pl.when(t == 1)
    def _():
        emit([halo[1], own[0], own[1]])


def upsample(halo, block, weight, bias):
    return pl.pallas_call(
        upsample_kernel,
        grid=(FT, 2),
        in_specs=[
            pl.BlockSpec((FT, RH, WD, CH), lambda t, s: (0, 0, 0, 0)),
            pl.BlockSpec((FT, RH, WD, CH), lambda t, s: (0, 0, 0, 0)),
            pl.BlockSpec((3, CH, CH), lambda t, s: (0, 0, s)),
            pl.BlockSpec((1, CH), lambda t, s: (0, s)),
        ],
        out_specs=pl.BlockSpec((1, 2 * RH, 2 * WD, CH), lambda t, s: (2 * t + s, 0, 0, 0)),
        out_shape=jax.ShapeDtypeStruct((2 * FT, 2 * RH, 2 * WD, CH), BF16),
        compiler_params=pltpu.CompilerParams(vmem_limit_bytes=LIMIT),
        cost_estimate=pl.CostEstimate(flops=3 * 10**9, bytes_accessed=12 * 10**6, transcendentals=0),
        name="upsample",
    )(halo, block, weight, bias)


def place_kernel(tokens_ref, line_ref, column_ref, out_ref):
    tokens = tokens_ref[...]
    line = line_ref[...]
    lines = out_ref.shape[0] * RH
    count = tokens.shape[1]
    zero = jnp.zeros_like(tokens)
    column = lax.broadcasted_iota(jnp.int32, (128, count), 0) == column_ref[...]
    column = column.astype(F32).astype(BF16)
    for t in range(FT):
        rows = [jnp.where(line == t * lines + h, tokens, zero) for h in range(lines)]
        placed = lax.dot_general(jnp.concatenate(rows, axis=0), column, NT, preferred_element_type=F32)
        placed = placed.astype(BF16).reshape(lines, ZC, 128)
        for g in range(out_ref.shape[0]):
            first = RH * g - 2
            for i in range(RH + 4):
                if 0 <= first + i < lines:
                    out_ref[g, t, i] = placed[first + i]
                else:
                    out_ref[g, t, i] = jnp.zeros((ZC, 128), BF16)


def latent_field(tokens, token_pos):
    tiles = lax.axis_size("height")
    slab = lax.axis_index("frame")
    count = tokens.shape[1]
    places = lax.dynamic_slice_in_dim(token_pos, lax.axis_index("height") * count, count, 0)
    line = places // WD - slab * (FT * RH * tiles)
    column = places % WD + 1
    grids = pl.pallas_call(
        place_kernel,
        in_specs=[VMEM] * 3,
        out_specs=VMEM,
        out_shape=jax.ShapeDtypeStruct((tiles, FT, RH + 4, ZC, 128), BF16),
        compiler_params=pltpu.CompilerParams(vmem_limit_bytes=LIMIT),
        cost_estimate=pl.CostEstimate(flops=3 * 10**8, bytes_accessed=10**6, transcendentals=0),
        name="place_tokens",
    )(tokens, line.reshape(1, count), column.reshape(1, count))
    grids = lax.all_to_all(grids, "height", 0, 0, tiled=True)
    own = jnp.sum(grids.astype(F32), axis=0).astype(BF16)
    return along(own, "frame", 2), along(own, "frame", 1), own


def on_device(
    tokens,
    token_pos,
    weight_in,
    bias_in,
    gain_one,
    offset_one,
    weight_one,
    bias_one,
    gain_two,
    offset_two,
    weight_two,
    bias_two,
    weight_time,
    bias_time,
):
    devices = lax.axis_size("frame") * lax.axis_size("height")
    slab, tile = lax.axis_index("frame"), lax.axis_index("height")
    side = 4
    in_x, in_y = slab % side, slab // side
    place = jnp.stack([tile // 2, tile % 2, in_x, in_y]).astype(jnp.int32)

    def send_x(v, k):
        return lax.ppermute(v, "frame", [(side * y + x, side * y + (x + k) % side) for y in range(4) for x in range(4)])

    def send_y(v, k):
        return lax.ppermute(v, "frame", [(side * y + x, side * ((y + k) % side) + x) for y in range(4) for x in range(4)])

    def unit_of(weight, low, high):
        unit = jnp.transpose(weight[:, :, low:high], (2, 0, 1, 4, 3))
        return unit.reshape(-1, 3, unit.shape[3], CH)

    def gathered(weight, low, high):
        return lax.all_gather(jnp.swapaxes(weight[:, :, low:high], 3, 4), "height", axis=3, tiled=True)

    def plan_of(low, high):
        return [(0, e - low, 3, e, 0, CH, None) for e in range(low, high)]

    rest, plan = ring_plan(*ring_gather(unit_of(weight_one, 2, 3), send_x, in_x), [2], 2, 1)
    kernel_one = ([gathered(weight_one, 0, 2), *rest], plan_of(0, 2) + plan)
    rest, plan = ring_plan(*ring_gather(unit_of(weight_two, 1, 3), send_y, in_y), [1, 2], 3, 1)
    kernel_two = ([gathered(weight_two, 0, 1), *rest], plan_of(0, 1) + plan)
    flags = jnp.stack([slab > 0, tile > 0, tile < lax.axis_size("height") - 1]).astype(F32)
    row = lambda v: v.reshape(1, -1)

    latent = latent_field(tokens, token_pos)
    base, stat = input_conv(latent, weight_in.reshape(-1, CH), row(bias_in), devices)

    def edges(j):
        return [1] if j == 0 else [2] if j == RH + 1 else []

    everything = lambda i, j: ([0] if i < FT else []) + edges(j)
    inner, stat = block_conv(
        "conv_one",
        [base],
        [(0, 2 * FT, 0, RH + 2, everything)],
        [(t, t + a, a) for t in range(FT) for a in range(3)],
        share_stats(stat),
        flags,
        place,
        row(gain_one),
        row(offset_one),
        kernel_one,
        {"bias": row(bias_one), "stat": None},
        BF16,
        devices,
    )
    behind = along(inner, "frame", 1)
    shared = share_stats(stat)

    def rows_around(v):
        return [along(v[:, RH - 1 :], "height", 1), v, along(v[:, :1], "height", -1)]

    pieces = lambda more: [
        (0, FT, 0, 1, lambda i, j: more + [1]),
        (0, FT, 1, RH, lambda i, j: more),
        (0, FT, RH + 1, 1, lambda i, j: more + [2]),
    ]
    (partial,) = block_conv(
        "conv_two_own",
        rows_around(inner),
        pieces([]),
        [(0, 0, 2), (1, 0, 1), (1, 1, 2)],
        shared,
        flags,
        place,
        row(gain_two),
        row(offset_two),
        kernel_two,
        {},
        F32,
        devices,
    )
    (block,) = block_conv(
        "conv_two_behind",
        rows_around(behind),
        pieces([0]),
        [(0, 0, 0), (0, 1, 1), (1, 1, 0)],
        shared,
        flags,
        place,
        row(gain_two),
        row(offset_two),
        kernel_two,
        {"partial": partial, "bias": row(bias_two), "base": base},
        BF16,
        devices,
    )
    return upsample(along(block, "frame", 1), block, weight_time, row(bias_time))


def solution(mesh):
    placed = (
        P(None, ("frame", "height")),
        P("frame"),
        P(),
        P(),
        P(),
        P(),
        P(None, None, None, None, "height"),
        P(),
        P(),
        P(),
        P(None, None, None, None, "height"),
        P(),
        P(),
        P(),
    )
    return jax.shard_map(
        on_device,
        mesh=mesh,
        in_specs=placed,
        out_specs=P("frame", "height", None, None),
        check_vma=False,
    )
```

```python
import functools

import jax
import jax.numpy as jnp
from jax import lax
from jax.experimental import pallas as pl
from jax.experimental.pallas import tpu as pltpu
from jax.sharding import PartitionSpec as P

GROUPS = 32
ZC = 16
FT = 2
RH = 4
WD = 104
WP = 112
CH = 512
CELLS = FT * RH * WD
F32 = jnp.float32
BF16 = jnp.bfloat16
NT = (((1,), (1,)), ((), ()))
TN = (((0,), (0,)), ((), ()))
VMEM = pl.BlockSpec(memory_space=pltpu.VMEM)
SMEM = pl.BlockSpec(memory_space=pltpu.SMEM)
ANY = pl.BlockSpec(memory_space=pl.ANY)
EXACT = lax.Precision.HIGHEST
LIMIT = 56 * 2**20


def along(value, axis, steps):
    count = lax.axis_size(axis)
    leading, last = (max(0, -steps), min(count, count - steps))
    return lax.ppermute(value, axis, [(source, source + steps) for source in range(leading, last)])


def spread(rows, cols, lanes_first, shift):
    one = lax.broadcasted_iota(jnp.int32, (rows, cols), 0)
    two = lax.broadcasted_iota(jnp.int32, (rows, cols), 1)
    lane, channel = (one, two) if lanes_first else (two, one)
    return (lane == channel // (CH // GROUPS) + shift).astype(F32)


def local_stats(values, stat_ref):
    cells = values.shape[0]
    total = jnp.broadcast_to(jnp.sum(values, axis=0, keepdims=True), (8, CH))
    size = cells * (CH // GROUPS)
    mean = jnp.dot(total, spread(CH, 128, False, 0), precision=EXACT, preferred_element_type=F32) / size
    per_channel = jnp.dot(mean, spread(128, CH, True, 0), precision=EXACT, preferred_element_type=F32)
    centered = values - per_channel[:1]
    square = jnp.broadcast_to(jnp.sum(centered * centered, axis=0, keepdims=True), (8, CH))
    spread_sq = jnp.dot(square, spread(CH, 128, False, GROUPS), precision=EXACT, preferred_element_type=F32)
    stat_ref[...] = jnp.broadcast_to((mean + spread_sq)[:1], stat_ref.shape)


def combine_stats(stats_ref, size):
    stats = stats_ref[...]
    devices = stats.shape[0]
    means = jnp.dot(stats, spread(128, CH, True, 0), precision=EXACT, preferred_element_type=F32)
    squares = jnp.dot(stats, spread(128, CH, True, GROUPS), precision=EXACT, preferred_element_type=F32)
    mean = jnp.sum(means, axis=0, keepdims=True) / devices
    away = means - mean
    total = jnp.sum(squares + size * (away * away), axis=0, keepdims=True)
    return mean, lax.rsqrt(total / (size * devices) + 1e-06)


def share_stats(stat):
    return lax.all_to_all(stat, ("frame", "height"), 0, 0, tiled=True)


def input_kernel(early_ref, behind_ref, own_ref, w_ref, bias_ref, base_ref, stat_ref):
    w = w_ref[...]
    lat = {}
    for k, ref in enumerate((early_ref, behind_ref, own_ref)):
        for i in range(FT):
            for r in range(RH + 4):
                value = ref[i, r].astype(F32)
                shifts = [value] + [pltpu.roll(value, 128 - e, 1) for e in (1, 2)]
                lat[k * FT + i, r] = jnp.concatenate([v.astype(BF16) for v in shifts], axis=0)
    for t in range(2 * FT):
        columns = []
        for r in range(RH + 2):
            columns.append(jnp.concatenate([lat[t + a, r + b] for a in range(3) for b in range(3)], axis=0))
        field = jnp.concatenate(columns, axis=1)
        total = lax.dot_general(field, w, TN, preferred_element_type=F32)
        total = (total + bias_ref[...]).astype(BF16).reshape(RH + 2, 128, CH)
        base_ref[t] = total[:, :WD]
    own = base_ref[FT:, 1 : RH + 1].reshape(CELLS, CH).astype(F32)
    local_stats(own, stat_ref)


def input_conv(latent, weight, bias, devices):
    return pl.pallas_call(
        input_kernel,
        in_specs=[VMEM] * 5,
        out_specs=[VMEM, VMEM],
        out_shape=[
            jax.ShapeDtypeStruct((2 * FT, RH + 2, WD, CH), BF16),
            jax.ShapeDtypeStruct((devices, 128), F32),
        ],
        compiler_params=pltpu.CompilerParams(vmem_limit_bytes=LIMIT),
        cost_estimate=pl.CostEstimate(flops=3 * 10**9, bytes_accessed=4 * 10**6, transcendentals=0),
        name="input_conv",
    )(*latent, weight, bias)


def after(value, earlier):
    return lax.optimization_barrier((value, earlier))[0]


def device_groups(inside, outside):
    sizes = {"y": 4, "x": 4, "z": 4, "c": 2}

    def walk(names, fixed):
        if not names:
            return [(fixed["y"] * 4 + fixed["x"]) * 8 + fixed["z"] * 2 + fixed["c"]]
        return [k for i in range(sizes[names[0]]) for k in walk(names[1:], {**fixed, names[0]: i})]

    def settings(names):
        if not names:
            return [{}]
        return [{**rest, names[0]: i} for i in range(sizes[names[0]]) for rest in settings(names[1:])]

    return [walk(inside, fixed) for fixed in settings(outside)]


def quarter_of(weight, low, high, pos):
    taps = jnp.swapaxes(weight, 3, 4)
    return lax.dynamic_slice(taps, (0, 0, low, 16 * pos, 0), (3, 3, high - low, 16, CH))


def gather_plane(quarter):
    return lax.all_gather(quarter, ("frame", "height"), axis_index_groups=device_groups("zxc", "y"))


def plane_plan(array, low, high):
    return [
        (array, 8 * z + 2 * x + c, e - low, e, ("fixed", 2 * z + c, x))
        for e in range(low, high)
        for z in range(4)
        for x in range(4)
        for c in range(2)
    ]


def ring_plan(array, low, high, flip, step):
    return [(array, z, e - low, e, (flip, z, step)) for e in range(low, high) for z in range(4)]


def conv_kernel(pieces, products, taps, plan, weights, extras, *refs):
    refs = list(refs)
    raws = [refs.pop(0) for _ in pieces]
    stats_ref, flags_ref, place_ref, gain_ref, offset_ref = [refs.pop(0) for _ in range(5)]
    w_refs = [refs.pop(0) for _ in range(weights)]
    partial_ref = refs.pop(0) if "partial" in extras else None
    bias_ref = refs.pop(0) if "bias" in extras else None
    base_ref = refs.pop(0) if "base" in extras else None
    out_ref = refs.pop(0)
    stat_ref = refs.pop(0) if "stat" in extras else None
    field, wbuf, acc, sems = refs
    low, high = taps[0], taps[-1] + 1
    core, ring = place_ref[0], place_ref[1]
    columns = sorted({copy[3] for copy in plan})
    for array, index, source_e, e, (kind, block, quarter) in plan:
        if kind != "fixed":
            block = 2 * block + (1 - core if kind == "other" else core)
            quarter = lax.rem(ring + quarter, 4)
        rows = pl.multiple_of(block * 64 + quarter * 16, 16)
        source = w_refs[array].at[index, pl.ds(low, high - low), :, source_e]
        pltpu.make_async_copy(source, wbuf.at[columns.index(e), :, :, pl.ds(rows, 16)], sems.at[columns.index(e)]).start()
    mean, inverse = combine_stats(stats_ref, CELLS * (CH // GROUPS))
    scale = inverse * gain_ref[...]
    offset = offset_ref[...]
    for raw, (frame, frames, row, rows, flag_of) in zip(raws, pieces):
        for i in range(frames):
            for j in range(rows):
                value = (raw[i, j].astype(F32) - mean) * scale + offset
                half = 0.5 * value
                value = half + half * jnp.tanh(half)
                for which in flag_of(i, j):
                    value = value * flags_ref[which]
                field[frame + i, row + j, :WD] = value.astype(BF16)
                field[frame + i, row + j, WD:] = jnp.zeros((WP - WD, CH), BF16)
    total = jnp.zeros((FT * RH * WP, CH), F32)
    edge = jnp.zeros((1, CH), F32)
    for e, column in enumerate(columns):
        pltpu.make_async_copy(wbuf.at[e], wbuf.at[e], sems.at[e]).wait()
        for t in range(FT):
            terms = [(f, a) for (out, f, a) in products if out == t]
            xs = [field[f, b : b + RH].reshape(RH * WP, CH) for f, a in terms for b in range(3)]
            ws = [wbuf[e, a - low, b] for f, a in terms for b in range(3)]
            acc[e, pl.ds(t * RH * WP, RH * WP)] = lax.dot_general(
                jnp.concatenate(xs, axis=1), jnp.concatenate(ws, axis=1), NT, preferred_element_type=F32
            )
    for e, column in enumerate(columns):
        if column == 0:
            total = total + jnp.concatenate([edge, acc[e, :-1]], axis=0)
        elif column == 1:
            total = total + acc[e]
        else:
            total = total + jnp.concatenate([acc[e, 1:], edge], axis=0)
    total = total.reshape(FT, RH, WP, CH)[:, :, :WD]
    if partial_ref is not None:
        total = total + partial_ref[...]
    if bias_ref is not None:
        total = total + bias_ref[...]
    if base_ref is not None:
        total = total + base_ref[FT:, 1 : RH + 1].astype(F32)
    out_ref[...] = total.astype(out_ref.dtype)
    if stat_ref is not None:
        local_stats(total.astype(BF16).astype(F32).reshape(CELLS, CH), stat_ref)


def block_conv(name, raws, pieces, products, stats, flags, place, gain, offset, weight, extras, kind, devices):
    arrays, plan = weight
    columns = len({copy[3] for copy in plan})
    taps = sorted({a for _, _, a in products})
    frames = max(f for _, f, _ in products) + 1
    args = [*raws, stats, flags, place, gain, offset, *arrays]
    args += [extras[k] for k in ("partial", "bias", "base") if k in extras]
    specs = [*[VMEM] * len(raws), VMEM, SMEM, SMEM, VMEM, VMEM, *[ANY] * len(arrays)]
    specs += [VMEM] * (len(args) - len(specs))
    shapes = [jax.ShapeDtypeStruct((FT, RH, WD, CH), kind)]
    if "stat" in extras:
        shapes.append(jax.ShapeDtypeStruct((devices, 128), F32))
    return pl.pallas_call(
        functools.partial(conv_kernel, pieces, products, taps, plan, len(arrays), tuple(extras)),
        in_specs=specs,
        out_specs=[VMEM] * len(shapes),
        out_shape=shapes,
        scratch_shapes=[
            pltpu.VMEM((frames, RH + 2, WP, CH), BF16),
            pltpu.VMEM((columns, len(taps), 3, CH, CH), BF16),
            pltpu.VMEM((columns, FT * RH * WP, CH), F32),
            pltpu.SemaphoreType.DMA((columns,)),
        ],
        compiler_params=pltpu.CompilerParams(vmem_limit_bytes=LIMIT),
        cost_estimate=pl.CostEstimate(
            flops=len(products) * 2 * 3 * columns * RH * WP * CH * CH, bytes_accessed=16 * 10**6, transcendentals=0
        ),
        name=name,
    )(*args)


def upsample_kernel(halo_ref, block_ref, w_ref, bias_ref, out_ref):
    t = pl.program_id(0)
    s = pl.program_id(1)
    cells = RH * WD
    halo = [halo_ref[i].reshape(cells, CH) for i in range(FT)]
    own = [block_ref[i].reshape(cells, CH) for i in range(FT)]

    def emit(parts):
        field = jnp.concatenate(parts, axis=1)
        w = w_ref[...].reshape(3 * CH, CH)
        total = jnp.dot(field, w, preferred_element_type=F32) + bias_ref[...]
        total = total.astype(BF16).reshape(RH, WD, CH)
        twice = lax.broadcasted_iota(jnp.int32, (2 * WD, WD), 0) // 2 == lax.broadcasted_iota(jnp.int32, (2 * WD, WD), 1)
        twice = twice.astype(F32).astype(BF16)
        for r in range(RH):
            wide = jnp.dot(twice, total[r], preferred_element_type=F32).astype(BF16)
            out_ref[0, 2 * r] = wide
            out_ref[0, 2 * r + 1] = wide

    @pl.when(t == 0)
    def _():
        emit([halo[0], halo[1], own[0]])

    @pl.when(t == 1)
    def _():
        emit([halo[1], own[0], own[1]])


def upsample(halo, block, weight, bias):
    return pl.pallas_call(
        upsample_kernel,
        grid=(FT, 2),
        in_specs=[
            pl.BlockSpec((FT, RH, WD, CH), lambda t, s: (0, 0, 0, 0)),
            pl.BlockSpec((FT, RH, WD, CH), lambda t, s: (0, 0, 0, 0)),
            pl.BlockSpec((3, CH, CH), lambda t, s: (0, 0, s)),
            pl.BlockSpec((1, CH), lambda t, s: (0, s)),
        ],
        out_specs=pl.BlockSpec((1, 2 * RH, 2 * WD, CH), lambda t, s: (2 * t + s, 0, 0, 0)),
        out_shape=jax.ShapeDtypeStruct((2 * FT, 2 * RH, 2 * WD, CH), BF16),
        compiler_params=pltpu.CompilerParams(vmem_limit_bytes=LIMIT),
        cost_estimate=pl.CostEstimate(flops=3 * 10**9, bytes_accessed=12 * 10**6, transcendentals=0),
        name="upsample",
    )(halo, block, weight, bias)


def place_kernel(tokens_ref, line_ref, column_ref, out_ref):
    tokens = tokens_ref[...]
    line = line_ref[...]
    lines = out_ref.shape[0] * RH
    count = tokens.shape[1]
    zero = jnp.zeros_like(tokens)
    column = lax.broadcasted_iota(jnp.int32, (128, count), 0) == column_ref[...]
    column = column.astype(F32).astype(BF16)
    for t in range(FT):
        rows = [jnp.where(line == t * lines + h, tokens, zero) for h in range(lines)]
        placed = lax.dot_general(jnp.concatenate(rows, axis=0), column, NT, preferred_element_type=F32)
        placed = placed.astype(BF16).reshape(lines, ZC, 128)
        for g in range(out_ref.shape[0]):
            first = RH * g - 2
            for i in range(RH + 4):
                if 0 <= first + i < lines:
                    out_ref[g, t, i] = placed[first + i]
                else:
                    out_ref[g, t, i] = jnp.zeros((ZC, 128), BF16)


def latent_field(tokens, token_pos):
    tiles = lax.axis_size("height")
    slab = lax.axis_index("frame")
    count = tokens.shape[1]
    places = lax.dynamic_slice_in_dim(token_pos, lax.axis_index("height") * count, count, 0)
    line = places // WD - slab * (FT * RH * tiles)
    column = places % WD + 1
    grids = pl.pallas_call(
        place_kernel,
        in_specs=[VMEM] * 3,
        out_specs=VMEM,
        out_shape=jax.ShapeDtypeStruct((tiles, FT, RH + 4, ZC, 128), BF16),
        compiler_params=pltpu.CompilerParams(vmem_limit_bytes=LIMIT),
        cost_estimate=pl.CostEstimate(flops=3 * 10**8, bytes_accessed=10**6, transcendentals=0),
        name="place_tokens",
    )(tokens, line.reshape(1, count), column.reshape(1, count))
    grids = lax.all_to_all(grids, "height", 0, 0, tiled=True)
    own = jnp.sum(grids.astype(F32), axis=0).astype(BF16)
    return along(own, "frame", 2), along(own, "frame", 1), own


def on_device(
    tokens,
    token_pos,
    weight_in,
    bias_in,
    gain_one,
    offset_one,
    weight_one,
    bias_one,
    gain_two,
    offset_two,
    weight_two,
    bias_two,
    weight_time,
    bias_time,
):
    devices = lax.axis_size("frame") * lax.axis_size("height")
    slab, tile = lax.axis_index("frame"), lax.axis_index("height")
    in_x, in_y = slab % 4, slab // 4
    place = jnp.stack([tile % 2, in_y]).astype(jnp.int32)
    flags = jnp.stack([slab > 0, tile > 0, tile < lax.axis_size("height") - 1]).astype(F32)
    row = lambda v: v.reshape(1, -1)

    def send_y(v, k):
        return lax.ppermute(v, "frame", [(4 * y + x, 4 * ((y + k) % 4) + x) for y in range(4) for x in range(4)])

    def swap_core(v):
        return lax.ppermute(v, "height", [(i, i ^ 1) for i in range(8)])

    near = lax.all_gather(
        quarter_of(weight_two, 1, 3, in_y), ("frame", "height"), axis_index_groups=device_groups("z", "yxc")
    )
    one_a = gather_plane(after(quarter_of(weight_one, 0, 2, in_x), near))
    one_b = gather_plane(after(quarter_of(weight_one, 2, 3, in_x), near))
    two_a = gather_plane(after(quarter_of(weight_two, 0, 1, in_x), near))

    latent = latent_field(tokens, token_pos)
    near = after(near, latent[2])
    left, right = send_y(near, 1), send_y(near, -1)
    base, stat = input_conv(latent, weight_in.reshape(-1, CH), row(bias_in), devices)
    shared = share_stats(stat)
    far = send_y(after(left, shared), 1)

    def edges(j):
        return [1] if j == 0 else [2] if j == RH + 1 else []

    everything = lambda i, j: ([0] if i < FT else []) + edges(j)
    norm_one = (shared, flags, place, row(gain_one), row(offset_one))
    common = ([base], [(0, 2 * FT, 0, RH + 2, everything)], [(t, t + a, a) for t in range(FT) for a in range(3)])
    (partial,) = block_conv(
        "conv_one_first", *common, *norm_one, ([one_a], plane_plan(0, 0, 2)), {}, F32, devices
    )
    swapped = [swap_core(after(v, shared)) for v in (near, left, right)]
    inner, stat = block_conv(
        "conv_one_last",
        *common,
        *norm_one,
        ([one_b], plane_plan(0, 2, 3)),
        {"partial": partial, "bias": row(bias_one), "stat": None},
        BF16,
        devices,
    )
    shared = share_stats(stat)
    behind = along(inner, "frame", 1)
    swapped.append(swap_core(after(far, inner)))
    arrays = [two_a, near, left, right, far, *swapped]
    plan = plane_plan(0, 0, 1)
    for k, step in enumerate((0, 3, 1, 2)):
        plan += ring_plan(1 + k, 1, 3, "own", step) + ring_plan(5 + k, 1, 3, "other", step)
    kernel_two = (arrays, plan)
    norm_two = (shared, flags, place, row(gain_two), row(offset_two))

    def rows_around(v):
        return [along(v[:, RH - 1 :], "height", 1), v, along(v[:, :1], "height", -1)]

    pieces = lambda more: [
        (0, FT, 0, 1, lambda i, j: more + [1]),
        (0, FT, 1, RH, lambda i, j: more),
        (0, FT, RH + 1, 1, lambda i, j: more + [2]),
    ]
    (partial,) = block_conv(
        "conv_two_own",
        rows_around(inner),
        pieces([]),
        [(0, 0, 2), (1, 0, 1), (1, 1, 2)],
        *norm_two,
        kernel_two,
        {},
        F32,
        devices,
    )
    (block,) = block_conv(
        "conv_two_behind",
        rows_around(behind),
        pieces([0]),
        [(0, 0, 0), (0, 1, 1), (1, 1, 0)],
        *norm_two,
        kernel_two,
        {"partial": partial, "bias": row(bias_two), "base": base},
        BF16,
        devices,
    )
    return upsample(along(block, "frame", 1), block, weight_time, row(bias_time))


def solution(mesh):
    placed = (
        P(None, ("frame", "height")),
        P("frame"),
        P(),
        P(),
        P(),
        P(),
        P(None, None, None, None, "height"),
        P(),
        P(),
        P(),
        P(None, None, None, None, "height"),
        P(),
        P(),
        P(),
    )
    return jax.shard_map(
        on_device,
        mesh=mesh,
        in_specs=placed,
        out_specs=P("frame", "height", None, None),
        check_vma=False,
    )
```

```python
import functools

import jax
import jax.numpy as jnp
from jax import lax
from jax.experimental import pallas as pl
from jax.experimental.pallas import tpu as pltpu
from jax.sharding import PartitionSpec as P

GROUPS = 32
ZC = 16
FT = 2
RH = 4
WD = 104
WP = 112
CH = 512
CELLS = FT * RH * WD
F32 = jnp.float32
BF16 = jnp.bfloat16
NT = (((1,), (1,)), ((), ()))
TN = (((0,), (0,)), ((), ()))
VMEM = pl.BlockSpec(memory_space=pltpu.VMEM)
SMEM = pl.BlockSpec(memory_space=pltpu.SMEM)
ANY = pl.BlockSpec(memory_space=pl.ANY)
EXACT = lax.Precision.HIGHEST
LIMIT = 56 * 2**20


def along(value, axis, steps):
    count = lax.axis_size(axis)
    leading, last = (max(0, -steps), min(count, count - steps))
    return lax.ppermute(value, axis, [(source, source + steps) for source in range(leading, last)])


def spread(rows, cols, lanes_first, shift):
    one = lax.broadcasted_iota(jnp.int32, (rows, cols), 0)
    two = lax.broadcasted_iota(jnp.int32, (rows, cols), 1)
    lane, channel = (one, two) if lanes_first else (two, one)
    return (lane == channel // (CH // GROUPS) + shift).astype(F32)


def local_stats(values, stat_ref):
    cells = values.shape[0]
    total = jnp.broadcast_to(jnp.sum(values, axis=0, keepdims=True), (8, CH))
    size = cells * (CH // GROUPS)
    mean = jnp.dot(total, spread(CH, 128, False, 0), precision=EXACT, preferred_element_type=F32) / size
    per_channel = jnp.dot(mean, spread(128, CH, True, 0), precision=EXACT, preferred_element_type=F32)
    centered = values - per_channel[:1]
    square = jnp.broadcast_to(jnp.sum(centered * centered, axis=0, keepdims=True), (8, CH))
    spread_sq = jnp.dot(square, spread(CH, 128, False, GROUPS), precision=EXACT, preferred_element_type=F32)
    stat_ref[...] = jnp.broadcast_to((mean + spread_sq)[:1], stat_ref.shape)


def combine_stats(stats_ref, size):
    stats = stats_ref[...]
    devices = stats.shape[0]
    means = jnp.dot(stats, spread(128, CH, True, 0), precision=EXACT, preferred_element_type=F32)
    squares = jnp.dot(stats, spread(128, CH, True, GROUPS), precision=EXACT, preferred_element_type=F32)
    mean = jnp.sum(means, axis=0, keepdims=True) / devices
    away = means - mean
    total = jnp.sum(squares + size * (away * away), axis=0, keepdims=True)
    return mean, lax.rsqrt(total / (size * devices) + 1e-06)


def share_stats(stat):
    return lax.all_to_all(stat, ("frame", "height"), 0, 0, tiled=True)


def input_kernel(early_ref, behind_ref, own_ref, w_ref, bias_ref, base_ref, stat_ref):
    w = w_ref[...]
    lat = {}
    for k, ref in enumerate((early_ref, behind_ref, own_ref)):
        for i in range(FT):
            for r in range(RH + 4):
                value = ref[i, r].astype(F32)
                shifts = [value] + [pltpu.roll(value, 128 - e, 1) for e in (1, 2)]
                lat[k * FT + i, r] = jnp.concatenate([v.astype(BF16) for v in shifts], axis=0)
    for t in range(2 * FT):
        columns = []
        for r in range(RH + 2):
            columns.append(jnp.concatenate([lat[t + a, r + b] for a in range(3) for b in range(3)], axis=0))
        field = jnp.concatenate(columns, axis=1)
        total = lax.dot_general(field, w, TN, preferred_element_type=F32)
        total = (total + bias_ref[...]).astype(BF16).reshape(RH + 2, 128, CH)
        base_ref[t] = total[:, :WD]
    own = base_ref[FT:, 1 : RH + 1].reshape(CELLS, CH).astype(F32)
    local_stats(own, stat_ref)


def input_conv(latent, weight, bias, devices):
    return pl.pallas_call(
        input_kernel,
        in_specs=[VMEM] * 5,
        out_specs=[VMEM, VMEM],
        out_shape=[
            jax.ShapeDtypeStruct((2 * FT, RH + 2, WD, CH), BF16),
            jax.ShapeDtypeStruct((devices, 128), F32),
        ],
        compiler_params=pltpu.CompilerParams(vmem_limit_bytes=LIMIT),
        cost_estimate=pl.CostEstimate(flops=3 * 10**9, bytes_accessed=4 * 10**6, transcendentals=0),
        name="input_conv",
    )(*latent, weight, bias)


def after(value, earlier):
    return lax.optimization_barrier((value, earlier))[0]


def quarter_of(weight, low, high, pos):
    taps = jnp.swapaxes(weight, 3, 4)
    return lax.dynamic_slice(taps, (0, 0, low, 16 * pos, 0), (3, 3, high - low, 16, CH))


def stack_kernel(*refs):
    *parts, out_ref, sems = refs
    copies = [pltpu.make_async_copy(part, out_ref.at[k], sems.at[k]) for k, part in enumerate(parts)]
    for copy in copies:
        copy.start()
    for copy in copies:
        copy.wait()


def stack(parts):
    return pl.pallas_call(
        stack_kernel,
        in_specs=[ANY] * len(parts),
        out_specs=ANY,
        out_shape=jax.ShapeDtypeStruct((len(parts), *parts[0].shape), parts[0].dtype),
        scratch_shapes=[pltpu.SemaphoreType.DMA((len(parts),))],
        cost_estimate=pl.CostEstimate(flops=0, bytes_accessed=4 * 10**6, transcendentals=0),
        name="stack_parts",
    )(*parts)


def gather_columns(weight, low, high):
    return lax.all_gather(jnp.swapaxes(weight[:, :, low:high], 3, 4), "height", axis=3, tiled=True)


def whole_plan(array, low, high):
    return [(array, None, e - low, e, ("whole", 0, 0)) for e in range(low, high)]


Z_SHIFTS = (0, 3, 1, 2)


def ring_plan(array, low, high, flip, step):
    return [(array, k, e - low, e, (flip, z, step)) for e in range(low, high) for k, z in enumerate(Z_SHIFTS)]


def conv_kernel(pieces, products, taps, plan, weights, extras, *refs):
    refs = list(refs)
    raws = [refs.pop(0) for _ in pieces]
    stats_ref, flags_ref, place_ref, gain_ref, offset_ref = [refs.pop(0) for _ in range(5)]
    w_refs = [refs.pop(0) for _ in range(weights)]
    partial_ref = refs.pop(0) if "partial" in extras else None
    bias_ref = refs.pop(0) if "bias" in extras else None
    base_ref = refs.pop(0) if "base" in extras else None
    out_ref = refs.pop(0)
    stat_ref = refs.pop(0) if "stat" in extras else None
    field, wbuf, acc, sems = refs
    low, high = taps[0], taps[-1] + 1
    core, ring, z = place_ref[0], place_ref[1], place_ref[2]
    columns = sorted({copy[3] for copy in plan})
    for array, index, source_e, e, (kind, shift, step) in plan:
        slot = columns.index(e)
        if kind == "whole":
            source, target = w_refs[array].at[pl.ds(low, high - low), :, source_e], wbuf.at[slot]
        else:
            block = 2 * lax.rem(z + shift, 4) + (1 - core if kind == "other" else core)
            rows = pl.multiple_of(block * 64 + lax.rem(ring + step, 4) * 16, 16)
            source = w_refs[array].at[index, pl.ds(low, high - low), :, source_e]
            target = wbuf.at[slot, :, :, pl.ds(rows, 16)]
        pltpu.make_async_copy(source, target, sems.at[slot]).start()
    mean, inverse = combine_stats(stats_ref, CELLS * (CH // GROUPS))
    scale = inverse * gain_ref[...]
    offset = offset_ref[...]
    for raw, (frame, frames, row, rows, flag_of) in zip(raws, pieces):
        for i in range(frames):
            for j in range(rows):
                value = (raw[i, j].astype(F32) - mean) * scale + offset
                half = 0.5 * value
                value = half + half * jnp.tanh(half)
                for which in flag_of(i, j):
                    value = value * flags_ref[which]
                field[frame + i, row + j, :WD] = value.astype(BF16)
                field[frame + i, row + j, WD:] = jnp.zeros((WP - WD, CH), BF16)
    total = jnp.zeros((FT * RH * WP, CH), F32)
    edge = jnp.zeros((1, CH), F32)
    for e, column in enumerate(columns):
        pltpu.make_async_copy(wbuf.at[e], wbuf.at[e], sems.at[e]).wait()
        for t in range(FT):
            terms = [(f, a) for (out, f, a) in products if out == t]
            xs = [field[f, b : b + RH].reshape(RH * WP, CH) for f, a in terms for b in range(3)]
            ws = [wbuf[e, a - low, b] for f, a in terms for b in range(3)]
            acc[e, pl.ds(t * RH * WP, RH * WP)] = lax.dot_general(
                jnp.concatenate(xs, axis=1), jnp.concatenate(ws, axis=1), NT, preferred_element_type=F32
            )
    for e, column in enumerate(columns):
        if column == 0:
            total = total + jnp.concatenate([edge, acc[e, :-1]], axis=0)
        elif column == 1:
            total = total + acc[e]
        else:
            total = total + jnp.concatenate([acc[e, 1:], edge], axis=0)
    total = total.reshape(FT, RH, WP, CH)[:, :, :WD]
    if partial_ref is not None:
        total = total + partial_ref[...]
    if bias_ref is not None:
        total = total + bias_ref[...]
    if base_ref is not None:
        total = total + base_ref[FT:, 1 : RH + 1].astype(F32)
    out_ref[...] = total.astype(out_ref.dtype)
    if stat_ref is not None:
        local_stats(total.astype(BF16).astype(F32).reshape(CELLS, CH), stat_ref)


def block_conv(name, raws, pieces, products, stats, flags, place, gain, offset, weight, extras, kind, devices):
    arrays, plan = weight
    columns = len({copy[3] for copy in plan})
    taps = sorted({a for _, _, a in products})
    frames = max(f for _, f, _ in products) + 1
    args = [*raws, stats, flags, place, gain, offset, *arrays]
    args += [extras[k] for k in ("partial", "bias", "base") if k in extras]
    specs = [*[VMEM] * len(raws), VMEM, SMEM, SMEM, VMEM, VMEM, *[ANY] * len(arrays)]
    specs += [VMEM] * (len(args) - len(specs))
    shapes = [jax.ShapeDtypeStruct((FT, RH, WD, CH), kind)]
    if "stat" in extras:
        shapes.append(jax.ShapeDtypeStruct((devices, 128), F32))
    return pl.pallas_call(
        functools.partial(conv_kernel, pieces, products, taps, plan, len(arrays), tuple(extras)),
        in_specs=specs,
        out_specs=[VMEM] * len(shapes),
        out_shape=shapes,
        scratch_shapes=[
            pltpu.VMEM((frames, RH + 2, WP, CH), BF16),
            pltpu.VMEM((columns, len(taps), 3, CH, CH), BF16),
            pltpu.VMEM((columns, FT * RH * WP, CH), F32),
            pltpu.SemaphoreType.DMA((columns,)),
        ],
        compiler_params=pltpu.CompilerParams(vmem_limit_bytes=LIMIT),
        cost_estimate=pl.CostEstimate(
            flops=len(products) * 2 * 3 * columns * RH * WP * CH * CH, bytes_accessed=16 * 10**6, transcendentals=0
        ),
        name=name,
    )(*args)


def upsample_kernel(halo_ref, block_ref, w_ref, bias_ref, out_ref):
    t = pl.program_id(0)
    s = pl.program_id(1)
    cells = RH * WD
    halo = [halo_ref[i].reshape(cells, CH) for i in range(FT)]
    own = [block_ref[i].reshape(cells, CH) for i in range(FT)]

    def emit(parts):
        field = jnp.concatenate(parts, axis=1)
        w = w_ref[...].reshape(3 * CH, CH)
        total = jnp.dot(field, w, preferred_element_type=F32) + bias_ref[...]
        total = total.astype(BF16).reshape(RH, WD, CH)
        twice = lax.broadcasted_iota(jnp.int32, (2 * WD, WD), 0) // 2 == lax.broadcasted_iota(jnp.int32, (2 * WD, WD), 1)
        twice = twice.astype(F32).astype(BF16)
        for r in range(RH):
            wide = jnp.dot(twice, total[r], preferred_element_type=F32).astype(BF16)
            out_ref[0, 2 * r] = wide
            out_ref[0, 2 * r + 1] = wide

    @pl.when(t == 0)
    def _():
        emit([halo[0], halo[1], own[0]])

    @pl.when(t == 1)
    def _():
        emit([halo[1], own[0], own[1]])


def upsample(halo, block, weight, bias):
    return pl.pallas_call(
        upsample_kernel,
        grid=(FT, 2),
        in_specs=[
            pl.BlockSpec((FT, RH, WD, CH), lambda t, s: (0, 0, 0, 0)),
            pl.BlockSpec((FT, RH, WD, CH), lambda t, s: (0, 0, 0, 0)),
            pl.BlockSpec((3, CH, CH), lambda t, s: (0, 0, s)),
            pl.BlockSpec((1, CH), lambda t, s: (0, s)),
        ],
        out_specs=pl.BlockSpec((1, 2 * RH, 2 * WD, CH), lambda t, s: (2 * t + s, 0, 0, 0)),
        out_shape=jax.ShapeDtypeStruct((2 * FT, 2 * RH, 2 * WD, CH), BF16),
        compiler_params=pltpu.CompilerParams(vmem_limit_bytes=LIMIT),
        cost_estimate=pl.CostEstimate(flops=3 * 10**9, bytes_accessed=12 * 10**6, transcendentals=0),
        name="upsample",
    )(halo, block, weight, bias)


def place_kernel(tokens_ref, line_ref, column_ref, out_ref):
    tokens = tokens_ref[...]
    line = line_ref[...]
    lines = out_ref.shape[0] * RH
    count = tokens.shape[1]
    zero = jnp.zeros_like(tokens)
    column = lax.broadcasted_iota(jnp.int32, (128, count), 0) == column_ref[...]
    column = column.astype(F32).astype(BF16)
    for t in range(FT):
        rows = [jnp.where(line == t * lines + h, tokens, zero) for h in range(lines)]
        placed = lax.dot_general(jnp.concatenate(rows, axis=0), column, NT, preferred_element_type=F32)
        placed = placed.astype(BF16).reshape(lines, ZC, 128)
        for g in range(out_ref.shape[0]):
            first = RH * g - 2
            for i in range(RH + 4):
                if 0 <= first + i < lines:
                    out_ref[g, t, i] = placed[first + i]
                else:
                    out_ref[g, t, i] = jnp.zeros((ZC, 128), BF16)


def latent_field(tokens, token_pos):
    tiles = lax.axis_size("height")
    slab = lax.axis_index("frame")
    count = tokens.shape[1]
    places = lax.dynamic_slice_in_dim(token_pos, lax.axis_index("height") * count, count, 0)
    line = places // WD - slab * (FT * RH * tiles)
    column = places % WD + 1
    grids = pl.pallas_call(
        place_kernel,
        in_specs=[VMEM] * 3,
        out_specs=VMEM,
        out_shape=jax.ShapeDtypeStruct((tiles, FT, RH + 4, ZC, 128), BF16),
        compiler_params=pltpu.CompilerParams(vmem_limit_bytes=LIMIT),
        cost_estimate=pl.CostEstimate(flops=3 * 10**8, bytes_accessed=10**6, transcendentals=0),
        name="place_tokens",
    )(tokens, line.reshape(1, count), column.reshape(1, count))
    grids = lax.all_to_all(grids, "height", 0, 0, tiled=True)
    own = jnp.sum(grids.astype(F32), axis=0).astype(BF16)
    return along(own, "frame", 2), along(own, "frame", 1), own


def on_device(
    tokens,
    token_pos,
    weight_in,
    bias_in,
    gain_one,
    offset_one,
    weight_one,
    bias_one,
    gain_two,
    offset_two,
    weight_two,
    bias_two,
    weight_time,
    bias_time,
):
    devices = lax.axis_size("frame") * lax.axis_size("height")
    slab, tile = lax.axis_index("frame"), lax.axis_index("height")
    in_y = slab // 4
    place = jnp.stack([tile % 2, in_y, tile // 2]).astype(jnp.int32)
    flags = jnp.stack([slab > 0, tile > 0, tile < lax.axis_size("height") - 1]).astype(F32)
    row = lambda v: v.reshape(1, -1)

    def send_y(v, k):
        return lax.ppermute(v, "frame", [(4 * y + x, 4 * ((y + k) % 4) + x) for y in range(4) for x in range(4)])

    def swap_core(v):
        return lax.ppermute(v, "height", [(i, i ^ 1) for i in range(8)])

    def send_z(v, k):
        return lax.ppermute(v, "height", [(i, (i + 2 * k) % 8) for i in range(8)])

    quarter = quarter_of(weight_two, 1, 3, in_y)
    sent = [quarter, *[send_z(quarter, k) for k in (1, 3, 2)]]
    one = gather_columns(weight_one, 0, 3)
    latent = latent_field(tokens, token_pos)
    two = gather_columns(after(weight_two, latent[2]), 0, 1)
    near = stack([after(v, latent[2]) for v in sent])
    left, right = send_y(near, 1), send_y(near, -1)
    base, stat = input_conv(latent, weight_in.reshape(-1, CH), row(bias_in), devices)
    shared = share_stats(stat)
    far = send_y(after(left, shared), 1)
    swapped = [swap_core(after(v, shared)) for v in (near, left, right)]

    def edges(j):
        return [1] if j == 0 else [2] if j == RH + 1 else []

    everything = lambda i, j: ([0] if i < FT else []) + edges(j)
    norm_one = (shared, flags, place, row(gain_one), row(offset_one))
    common = ([base], [(0, 2 * FT, 0, RH + 2, everything)], [(t, t + a, a) for t in range(FT) for a in range(3)])
    inner, stat = block_conv(
        "conv_one",
        *common,
        *norm_one,
        ([one], whole_plan(0, 0, 3)),
        {"bias": row(bias_one), "stat": None},
        BF16,
        devices,
    )
    shared = share_stats(stat)
    behind = along(after(inner, shared), "frame", 1)
    swapped.append(swap_core(after(far, inner)))
    arrays = [two, near, left, right, far, *swapped]
    plan = whole_plan(0, 0, 1)
    for k, step in enumerate((0, 3, 1, 2)):
        plan += ring_plan(1 + k, 1, 3, "own", step) + ring_plan(5 + k, 1, 3, "other", step)
    kernel_two = (arrays, plan)
    norm_two = (shared, flags, place, row(gain_two), row(offset_two))

    def rows_around(v):
        return [along(v[:, RH - 1 :], "height", 1), v, along(v[:, :1], "height", -1)]

    pieces = lambda more: [
        (0, FT, 0, 1, lambda i, j: more + [1]),
        (0, FT, 1, RH, lambda i, j: more),
        (0, FT, RH + 1, 1, lambda i, j: more + [2]),
    ]
    (partial,) = block_conv(
        "conv_two_own",
        rows_around(inner),
        pieces([]),
        [(0, 0, 2), (1, 0, 1), (1, 1, 2)],
        *norm_two,
        kernel_two,
        {},
        F32,
        devices,
    )
    (block,) = block_conv(
        "conv_two_behind",
        rows_around(after(behind, partial)),
        pieces([0]),
        [(0, 0, 0), (0, 1, 1), (1, 1, 0)],
        *norm_two,
        kernel_two,
        {"partial": partial, "bias": row(bias_two), "base": base},
        BF16,
        devices,
    )
    return upsample(along(block, "frame", 1), block, weight_time, row(bias_time))


def solution(mesh):
    placed = (
        P(None, ("frame", "height")),
        P("frame"),
        P(),
        P(),
        P(),
        P(),
        P(None, None, None, None, "height"),
        P(),
        P(),
        P(),
        P(None, None, None, None, "height"),
        P(),
        P(),
        P(),
    )
    return jax.shard_map(
        on_device,
        mesh=mesh,
        in_specs=placed,
        out_specs=P("frame", "height", None, None),
        check_vma=False,
    )
```

```python
import functools

import jax
import jax.numpy as jnp
from jax import lax
from jax.experimental import pallas as pl
from jax.experimental.pallas import tpu as pltpu
from jax.sharding import PartitionSpec as P

GROUPS = 32
ZC = 16
FT = 2
RH = 4
WD = 104
WP = 112
CH = 512
CELLS = FT * RH * WD
F32 = jnp.float32
BF16 = jnp.bfloat16
NT = (((1,), (1,)), ((), ()))
TN = (((0,), (0,)), ((), ()))
VMEM = pl.BlockSpec(memory_space=pltpu.VMEM)
SMEM = pl.BlockSpec(memory_space=pltpu.SMEM)
ANY = pl.BlockSpec(memory_space=pl.ANY)
EXACT = lax.Precision.HIGHEST
LIMIT = 56 * 2**20


def along(value, axis, steps):
    count = lax.axis_size(axis)
    leading, last = (max(0, -steps), min(count, count - steps))
    return lax.ppermute(value, axis, [(source, source + steps) for source in range(leading, last)])


def spread(rows, cols, lanes_first, shift):
    one = lax.broadcasted_iota(jnp.int32, (rows, cols), 0)
    two = lax.broadcasted_iota(jnp.int32, (rows, cols), 1)
    lane, channel = (one, two) if lanes_first else (two, one)
    return (lane == channel // (CH // GROUPS) + shift).astype(F32)


def local_stats(values, stat_ref):
    cells = values.shape[0]
    total = jnp.broadcast_to(jnp.sum(values, axis=0, keepdims=True), (8, CH))
    size = cells * (CH // GROUPS)
    mean = jnp.dot(total, spread(CH, 128, False, 0), precision=EXACT, preferred_element_type=F32) / size
    per_channel = jnp.dot(mean, spread(128, CH, True, 0), precision=EXACT, preferred_element_type=F32)
    centered = values - per_channel[:1]
    square = jnp.broadcast_to(jnp.sum(centered * centered, axis=0, keepdims=True), (8, CH))
    spread_sq = jnp.dot(square, spread(CH, 128, False, GROUPS), precision=EXACT, preferred_element_type=F32)
    stat_ref[...] = jnp.broadcast_to((mean + spread_sq)[:1], stat_ref.shape)


def combine_stats(stats_ref, size):
    stats = stats_ref[...]
    devices = stats.shape[0]
    means = jnp.dot(stats, spread(128, CH, True, 0), precision=EXACT, preferred_element_type=F32)
    squares = jnp.dot(stats, spread(128, CH, True, GROUPS), precision=EXACT, preferred_element_type=F32)
    mean = jnp.sum(means, axis=0, keepdims=True) / devices
    away = means - mean
    total = jnp.sum(squares + size * (away * away), axis=0, keepdims=True)
    return mean, lax.rsqrt(total / (size * devices) + 1e-06)


def share_stats(stat):
    return lax.all_to_all(stat, ("frame", "height"), 0, 0, tiled=True)


def input_kernel(early_ref, behind_ref, own_ref, w_ref, bias_ref, base_ref, stat_ref):
    w = w_ref[...]
    lat = {}
    for k, ref in enumerate((early_ref, behind_ref, own_ref)):
        for i in range(FT):
            for r in range(RH + 4):
                value = ref[i, r].astype(F32)
                shifts = [value] + [pltpu.roll(value, 128 - e, 1) for e in (1, 2)]
                lat[k * FT + i, r] = jnp.concatenate([v.astype(BF16) for v in shifts], axis=0)
    for t in range(2 * FT):
        columns = []
        for r in range(RH + 2):
            columns.append(jnp.concatenate([lat[t + a, r + b] for a in range(3) for b in range(3)], axis=0))
        field = jnp.concatenate(columns, axis=1)
        total = lax.dot_general(field, w, TN, preferred_element_type=F32)
        total = (total + bias_ref[...]).astype(BF16).reshape(RH + 2, 128, CH)
        base_ref[t] = total[:, :WD]
    own = base_ref[FT:, 1 : RH + 1].reshape(CELLS, CH).astype(F32)
    local_stats(own, stat_ref)


def input_conv(latent, weight, bias, devices):
    return pl.pallas_call(
        input_kernel,
        in_specs=[VMEM] * 5,
        out_specs=[VMEM, VMEM],
        out_shape=[
            jax.ShapeDtypeStruct((2 * FT, RH + 2, WD, CH), BF16),
            jax.ShapeDtypeStruct((devices, 128), F32),
        ],
        compiler_params=pltpu.CompilerParams(vmem_limit_bytes=LIMIT),
        cost_estimate=pl.CostEstimate(flops=3 * 10**9, bytes_accessed=4 * 10**6, transcendentals=0),
        name="input_conv",
    )(*latent, weight, bias)


def after(value, earlier):
    return lax.optimization_barrier((value, earlier))[0]


def quarter_kernel(one_ref, two_ref, place_ref, out_one, out_two, sems):
    copies = []
    for k in range(9):
        rows = pl.multiple_of(place_ref[3] * 16, 16)
        copies.append(pltpu.make_async_copy(one_ref.at[k % 3, :, k // 3, pl.ds(rows, 16)], out_one.at[k], sems.at[k]))
    for k in range(3):
        rows = pl.multiple_of(place_ref[1] * 16, 16)
        source = two_ref.at[k, :, 2, pl.ds(rows, 16)]
        copies.append(pltpu.make_async_copy(source, out_two.at[k], sems.at[9 + k]))
    for copy in copies:
        copy.start()
    for copy in copies:
        copy.wait()


def quarters_of(one, two, place):
    return pl.pallas_call(
        quarter_kernel,
        in_specs=[ANY, ANY, SMEM],
        out_specs=[VMEM] * 2,
        out_shape=[jax.ShapeDtypeStruct((n, 3, 16, CH), BF16) for n in (9, 3)],
        scratch_shapes=[pltpu.SemaphoreType.DMA((12,))],
        cost_estimate=pl.CostEstimate(flops=0, bytes_accessed=10**6, transcendentals=0),
        name="take_quarters",
    )(one, two, place)


def stack_kernel(*refs):
    *parts, out_ref, sems = refs
    copies = [pltpu.make_async_copy(part, out_ref.at[k], sems.at[k]) for k, part in enumerate(parts)]
    for copy in copies:
        copy.start()
    for copy in copies:
        copy.wait()


def stack(parts):
    return pl.pallas_call(
        stack_kernel,
        in_specs=[ANY] * len(parts),
        out_specs=VMEM,
        out_shape=jax.ShapeDtypeStruct((len(parts), *parts[0].shape), BF16),
        scratch_shapes=[pltpu.SemaphoreType.DMA((len(parts),))],
        compiler_params=pltpu.CompilerParams(vmem_limit_bytes=LIMIT),
        cost_estimate=pl.CostEstimate(flops=0, bytes_accessed=4 * 10**6, transcendentals=0),
        name="stack_parts",
    )(*parts)


def plane_groups():
    return [[(4 * y + x) * 8 + 2 * z + c for z in range(4) for x in range(4) for c in range(2)] for y in range(4)]


def plane_plan(array):
    return [
        (array, (8 * z + 2 * x + c, 3 * e), 0, 3, e, ("fixed", 2 * z + c, None, x))
        for e in range(3)
        for z in range(4)
        for x in range(4)
        for c in range(2)
    ]


def whole_plan(array, low, high):
    return [(array, e - low, 0, 3, e, ("whole", 0, None, 0)) for e in range(low, high)]


def shard_plan(array, kind):
    return [(array, e, 0, 3, e, (kind, 0, None, 0)) for e in (2,)]


Z_SHIFTS = (3, 1, 2)


def ring_plan(array, begin, end, kind, ring, step):
    plan = []
    k = begin
    while k < end:
        stop = min(end, k - k % 3 + 3)
        for i, z in enumerate(Z_SHIFTS):
            plan.append((array, (i, k - begin), k % 3, stop - k, k // 3, (kind, z, ring, step)))
        k = stop
    return plan


def conv_kernel(pieces, products, taps, plan, weights, extras, *refs):
    refs = list(refs)
    raws = [refs.pop(0) for _ in pieces]
    stats_ref, flags_ref, place_ref, gain_ref, offset_ref = [refs.pop(0) for _ in range(5)]
    w_refs = [refs.pop(0) for _ in range(weights)]
    partial_ref = refs.pop(0) if "partial" in extras else None
    bias_ref = refs.pop(0) if "bias" in extras else None
    base_ref = refs.pop(0) if "base" in extras else None
    out_ref = refs.pop(0)
    stat_ref = refs.pop(0) if "stat" in extras else None
    field, wbuf, acc, sems = refs
    low, high = taps[0], taps[-1] + 1
    core, z = place_ref[0], place_ref[2]
    columns = sorted({copy[4] for copy in plan})
    for array, index, tap, length, e, (kind, shift, ring, step) in plan:
        slot = columns.index(e)
        begin, end = max(tap, low), min(tap + length, high)
        if begin >= end:
            continue
        taps_of = pl.ds(begin - low, end - begin)
        if kind == "whole":
            source, target = w_refs[array].at[pl.ds(begin, end - begin), :, index], wbuf.at[slot, taps_of]
        else:
            block = 2 * lax.rem(z + shift, 4) + (1 - core if kind == "other" else core)
            rows, width = block * 64, 16
            if kind == "fixed":
                rows = 64 * shift + 16 * step
            elif ring is None:
                width = 64
            else:
                rows = rows + lax.rem(place_ref[ring] + step, 4) * 16
            if kind != "fixed" and ring is None:
                source = w_refs[array].at[pl.ds(begin, end - begin), :, index]
            else:
                source = w_refs[array].at[index[0], pl.ds(index[1] + begin - tap, end - begin)]
            target = wbuf.at[slot, taps_of, :, pl.ds(pl.multiple_of(rows, 16), width)]
        pltpu.make_async_copy(source, target, sems.at[slot]).start()
    mean, inverse = combine_stats(stats_ref, CELLS * (CH // GROUPS))
    scale = inverse * gain_ref[...]
    offset = offset_ref[...]
    for raw, (frame, frames, row, rows, flag_of) in zip(raws, pieces):
        for i in range(frames):
            for j in range(rows):
                value = (raw[i, j].astype(F32) - mean) * scale + offset
                half = 0.5 * value
                value = half + half * jnp.tanh(half)
                for which in flag_of(i, j):
                    value = value * flags_ref[which]
                field[frame + i, row + j, :WD] = value.astype(BF16)
                field[frame + i, row + j, WD:] = jnp.zeros((WP - WD, CH), BF16)
    total = jnp.zeros((FT * RH * WP, CH), F32)
    edge = jnp.zeros((1, CH), F32)
    for e, column in enumerate(columns):
        pltpu.make_async_copy(wbuf.at[e], wbuf.at[e], sems.at[e]).wait()
        for t in range(FT):
            terms = [(f, a) for (out, f, a) in products if out == t]
            xs = [field[f, b : b + RH].reshape(RH * WP, CH) for f, a in terms for b in range(3)]
            ws = [wbuf[e, a - low, b] for f, a in terms for b in range(3)]
            acc[e, pl.ds(t * RH * WP, RH * WP)] = lax.dot_general(
                jnp.concatenate(xs, axis=1), jnp.concatenate(ws, axis=1), NT, preferred_element_type=F32
            )
    for e, column in enumerate(columns):
        if column == 0:
            total = total + jnp.concatenate([edge, acc[e, :-1]], axis=0)
        elif column == 1:
            total = total + acc[e]
        else:
            total = total + jnp.concatenate([acc[e, 1:], edge], axis=0)
    total = total.reshape(FT, RH, WP, CH)[:, :, :WD]
    if partial_ref is not None:
        total = total + partial_ref[...]
    if bias_ref is not None:
        total = total + bias_ref[...]
    if base_ref is not None:
        total = total + base_ref[FT:, 1 : RH + 1].astype(F32)
    out_ref[...] = total.astype(out_ref.dtype)
    if stat_ref is not None:
        local_stats(total.astype(BF16).astype(F32).reshape(CELLS, CH), stat_ref)


def block_conv(name, raws, pieces, products, stats, flags, place, gain, offset, weight, extras, kind, devices):
    arrays, plan = weight
    columns = len({copy[4] for copy in plan})
    taps = sorted({a for _, _, a in products})
    frames = max(f for _, f, _ in products) + 1
    args = [*raws, stats, flags, place, gain, offset, *arrays]
    args += [extras[k] for k in ("partial", "bias", "base") if k in extras]
    specs = [*[VMEM] * len(raws), VMEM, SMEM, SMEM, VMEM, VMEM, *[ANY] * len(arrays)]
    specs += [VMEM] * (len(args) - len(specs))
    shapes = [jax.ShapeDtypeStruct((FT, RH, WD, CH), kind)]
    if "stat" in extras:
        shapes.append(jax.ShapeDtypeStruct((devices, 128), F32))
    return pl.pallas_call(
        functools.partial(conv_kernel, pieces, products, taps, plan, len(arrays), tuple(extras)),
        in_specs=specs,
        out_specs=[VMEM] * len(shapes),
        out_shape=shapes,
        scratch_shapes=[
            pltpu.VMEM((frames, RH + 2, WP, CH), BF16),
            pltpu.VMEM((columns, len(taps), 3, CH, CH), BF16),
            pltpu.VMEM((columns, FT * RH * WP, CH), F32),
            pltpu.SemaphoreType.DMA((columns,)),
        ],
        compiler_params=pltpu.CompilerParams(vmem_limit_bytes=LIMIT),
        cost_estimate=pl.CostEstimate(
            flops=len(products) * 2 * 3 * columns * RH * WP * CH * CH, bytes_accessed=16 * 10**6, transcendentals=0
        ),
        name=name,
    )(*args)


def upsample_kernel(halo_ref, block_ref, w_ref, bias_ref, out_ref):
    t = pl.program_id(0)
    s = pl.program_id(1)
    cells = RH * WD
    halo = [halo_ref[i].reshape(cells, CH) for i in range(FT)]
    own = [block_ref[i].reshape(cells, CH) for i in range(FT)]

    def emit(parts):
        field = jnp.concatenate(parts, axis=1)
        w = w_ref[...].reshape(3 * CH, CH)
        total = jnp.dot(field, w, preferred_element_type=F32) + bias_ref[...]
        total = total.astype(BF16).reshape(RH, WD, CH)
        twice = lax.broadcasted_iota(jnp.int32, (2 * WD, WD), 0) // 2 == lax.broadcasted_iota(jnp.int32, (2 * WD, WD), 1)
        twice = twice.astype(F32).astype(BF16)
        for r in range(RH):
            wide = jnp.dot(twice, total[r], preferred_element_type=F32).astype(BF16)
            out_ref[0, 2 * r] = wide
            out_ref[0, 2 * r + 1] = wide

    @pl.when(t == 0)
    def _():
        emit([halo[0], halo[1], own[0]])

    @pl.when(t == 1)
    def _():
        emit([halo[1], own[0], own[1]])


def upsample(halo, block, weight, bias):
    return pl.pallas_call(
        upsample_kernel,
        grid=(FT, 2),
        in_specs=[
            pl.BlockSpec((FT, RH, WD, CH), lambda t, s: (0, 0, 0, 0)),
            pl.BlockSpec((FT, RH, WD, CH), lambda t, s: (0, 0, 0, 0)),
            pl.BlockSpec((3, CH, CH), lambda t, s: (0, 0, s)),
            pl.BlockSpec((1, CH), lambda t, s: (0, s)),
        ],
        out_specs=pl.BlockSpec((1, 2 * RH, 2 * WD, CH), lambda t, s: (2 * t + s, 0, 0, 0)),
        out_shape=jax.ShapeDtypeStruct((2 * FT, 2 * RH, 2 * WD, CH), BF16),
        compiler_params=pltpu.CompilerParams(vmem_limit_bytes=LIMIT),
        cost_estimate=pl.CostEstimate(flops=3 * 10**9, bytes_accessed=12 * 10**6, transcendentals=0),
        name="upsample",
    )(halo, block, weight, bias)


def deal_kernel(tokens_ref, line_ref, column_ref, tile_ref, tile_down_ref, out_ref):
    tiles = out_ref.shape[0]
    count = tokens_ref.shape[1]
    tile = tile_ref[...]
    same = tile_down_ref[...] == tile
    earlier = lax.broadcasted_iota(jnp.int32, (count, count), 0) < lax.broadcasted_iota(jnp.int32, (count, count), 1)
    rank = jnp.sum((same & earlier).astype(F32), axis=0, keepdims=True)
    slot = tile * 128 + rank.astype(jnp.int32)
    onto = lax.broadcasted_iota(jnp.int32, (tiles * 128, count), 0) == slot
    rest = jnp.zeros((14, count), F32)
    value = [tokens_ref[...].astype(F32), line_ref[...].astype(F32), column_ref[...].astype(F32), rest]
    value = jnp.concatenate(value, axis=0).astype(BF16)
    dealt = lax.dot_general(value, onto.astype(F32).astype(BF16), NT, preferred_element_type=F32).astype(BF16)
    for g in range(tiles):
        for k in range(3):
            near = g + k - 1
            if 0 <= near < tiles:
                out_ref[g, k] = dealt[:, near * 128 : near * 128 + 128]
            else:
                out_ref[g, k] = jnp.zeros((32, 128), BF16)


def place_kernel(dealt_ref, first_ref, out_ref):
    blocks = [dealt_ref[i, k].astype(F32) for i in range(dealt_ref.shape[0]) for k in range(3)]
    dealt = jnp.concatenate(blocks, axis=1)
    value, line, column = dealt[:ZC], dealt[ZC : ZC + 1], dealt[ZC + 1 : ZC + 2]
    count = dealt.shape[1]
    first = first_ref[0]
    field = []
    for t in range(FT):
        for i in range(RH + 4):
            row = first + i
            wanted = jnp.where((row >= 0) & (row < 32), t * 32 + row, -1).astype(F32)
            field.append(jnp.where(line == wanted, value, 0.0))
    onto = lax.broadcasted_iota(jnp.int32, (128, count), 0).astype(F32) == column
    placed = lax.dot_general(
        jnp.concatenate(field, axis=0).astype(BF16), onto.astype(F32).astype(BF16), NT, preferred_element_type=F32
    )
    out_ref[...] = placed.astype(BF16).reshape(out_ref.shape)


def latent_own(tokens, token_pos):
    tiles = lax.axis_size("height")
    mine = lax.axis_index("height")
    count = tokens.shape[1]
    places = lax.dynamic_slice_in_dim(token_pos, mine * count, count, 0)
    line = places // WD - lax.axis_index("frame") * (FT * RH * tiles)
    column = places % WD + 1
    tile = line % (RH * tiles) // RH
    params = pltpu.CompilerParams(vmem_limit_bytes=LIMIT)
    cost = pl.CostEstimate(flops=3 * 10**8, bytes_accessed=10**6, transcendentals=0)
    across = lambda v: v.reshape(1, count)
    dealt = pl.pallas_call(
        deal_kernel,
        in_specs=[VMEM] * 5,
        out_specs=VMEM,
        out_shape=jax.ShapeDtypeStruct((tiles, 3, 32, 128), BF16),
        compiler_params=params,
        cost_estimate=cost,
        name="deal_tokens",
    )(tokens, across(line), across(column), across(tile), tile.reshape(count, 1))
    dealt = lax.all_to_all(dealt, "height", 0, 0, tiled=True)
    return pl.pallas_call(
        place_kernel,
        in_specs=[VMEM, SMEM],
        out_specs=VMEM,
        out_shape=jax.ShapeDtypeStruct((FT, RH + 4, ZC, 128), BF16),
        compiler_params=params,
        cost_estimate=cost,
        name="place_tokens",
    )(dealt, (mine * RH - 2).reshape(1).astype(jnp.int32))


def latent_slabs(own):
    return along(own, "frame", 2), along(own, "frame", 1), own


def on_device(
    tokens,
    token_pos,
    weight_in,
    bias_in,
    gain_one,
    offset_one,
    weight_one,
    bias_one,
    gain_two,
    offset_two,
    weight_two,
    bias_two,
    weight_time,
    bias_time,
):
    devices = lax.axis_size("frame") * lax.axis_size("height")
    slab, tile = lax.axis_index("frame"), lax.axis_index("height")
    place = jnp.stack([tile % 2, slab // 4, tile // 2, slab % 4]).astype(jnp.int32)
    flags = jnp.stack([slab > 0, tile > 0, tile < lax.axis_size("height") - 1]).astype(F32)
    row = lambda v: v.reshape(1, -1)

    def send_y(v, k):
        return lax.ppermute(v, "frame", [(4 * y + x, 4 * ((y + k) % 4) + x) for y in range(4) for x in range(4)])

    def swap_core(v):
        return lax.ppermute(v, "height", [(i, i ^ 1) for i in range(8)])

    def send_z(v, k):
        return lax.ppermute(v, "height", [(i, (i + 2 * k) % 8) for i in range(8)])

    shard_one, shard_two = jnp.swapaxes(weight_one, 3, 4), jnp.swapaxes(weight_two, 3, 4)
    quarter_one, quarter_two = quarters_of(shard_one, shard_two, place)
    one = lax.all_gather(quarter_one, ("frame", "height"), axis_index_groups=plane_groups())
    sent = [send_z(quarter_two, k) for k in (1, 3, 2)]
    own = latent_own(after(tokens, quarter_one), token_pos)
    latent = latent_slabs(own)
    near = stack([after(v, latent[0]) for v in sent])
    held = [send_y(near, k) if k else near for k in (0, 1, -1, 2)]
    base, stat = input_conv([after(v, near) for v in latent], weight_in.reshape(-1, CH), row(bias_in), devices)
    shared = share_stats(stat)
    two = lax.all_gather(after(shard_two, base)[:, :, :2], "height", axis=3, tiled=True)
    swapped = [swap_core(v) for v in held]

    def edges(j):
        return [1] if j == 0 else [2] if j == RH + 1 else []

    everything = lambda i, j: ([0] if i < FT else []) + edges(j)
    norm_one = (shared, flags, place, row(gain_one), row(offset_one))
    common = ([after(base, tuple(held))], [(0, 2 * FT, 0, RH + 2, everything)], [(t, t + a, a) for t in range(FT) for a in range(3)])
    inner, stat = block_conv(
        "conv_one",
        *common,
        *norm_one,
        ([one], plane_plan(0)),
        {"bias": row(bias_one), "stat": None},
        BF16,
        devices,
    )
    shared = share_stats(stat)
    behind = along(inner, "frame", 1)
    plan = whole_plan(0, 0, 2) + shard_plan(1, "own") + shard_plan(2, "other")
    for k, step in enumerate((0, 3, 1, 2)):
        plan += ring_plan(3 + k, 6, 9, "own", 1, step) + ring_plan(7 + k, 6, 9, "other", 1, step)
    kernel_two = ([two, shard_two, swap_core(after(shard_two, base)), *held, *swapped], plan)
    norm_two = (shared, flags, place, row(gain_two), row(offset_two))

    def rows_around(v):
        return [along(v[:, RH - 1 :], "height", 1), v, along(v[:, :1], "height", -1)]

    def pieces(frame, more):
        return [
            (frame, FT, 0, 1, lambda i, j: more + [1]),
            (frame, FT, 1, RH, lambda i, j: more),
            (frame, FT, RH + 1, 1, lambda i, j: more + [2]),
        ]

    (block,) = block_conv(
        "conv_two",
        rows_around(after(behind, shared)) + rows_around(inner),
        pieces(0, [0]) + pieces(FT, []),
        [(t, t + a, a) for t in range(FT) for a in range(3)],
        *norm_two,
        kernel_two,
        {"bias": row(bias_two), "base": base},
        BF16,
        devices,
    )
    return upsample(along(block, "frame", 1), block, weight_time, row(bias_time))


def solution(mesh):
    placed = (
        P(None, ("frame", "height")),
        P("frame"),
        P(),
        P(),
        P(),
        P(),
        P(None, None, None, None, "height"),
        P(),
        P(),
        P(),
        P(None, None, None, None, "height"),
        P(),
        P(),
        P(),
    )
    return jax.shard_map(
        on_device,
        mesh=mesh,
        in_specs=placed,
        out_specs=P("frame", "height", None, None),
        check_vma=False,
    )
```

```python
import functools

import jax
import jax.numpy as jnp
from jax import lax
from jax.experimental import pallas as pl
from jax.experimental.pallas import tpu as pltpu
from jax.sharding import PartitionSpec as P

GROUPS = 32
ZC = 16
FT = 2
RH = 4
WD = 104
WP = 112
CH = 512
CELLS = FT * RH * WD
F32 = jnp.float32
BF16 = jnp.bfloat16
NT = (((1,), (1,)), ((), ()))
TN = (((0,), (0,)), ((), ()))
VMEM = pl.BlockSpec(memory_space=pltpu.VMEM)
SMEM = pl.BlockSpec(memory_space=pltpu.SMEM)
ANY = pl.BlockSpec(memory_space=pl.ANY)
EXACT = lax.Precision.HIGHEST
LIMIT = 56 * 2**20


def along(value, axis, steps):
    count = lax.axis_size(axis)
    leading, last = (max(0, -steps), min(count, count - steps))
    return lax.ppermute(value, axis, [(source, source + steps) for source in range(leading, last)])


def spread(rows, cols, lanes_first, shift):
    one = lax.broadcasted_iota(jnp.int32, (rows, cols), 0)
    two = lax.broadcasted_iota(jnp.int32, (rows, cols), 1)
    lane, channel = (one, two) if lanes_first else (two, one)
    return (lane == channel // (CH // GROUPS) + shift).astype(F32)


def local_stats(values, stat_ref):
    cells = values.shape[0]
    total = jnp.broadcast_to(jnp.sum(values, axis=0, keepdims=True), (8, CH))
    size = cells * (CH // GROUPS)
    mean = jnp.dot(total, spread(CH, 128, False, 0), precision=EXACT, preferred_element_type=F32) / size
    per_channel = jnp.dot(mean, spread(128, CH, True, 0), precision=EXACT, preferred_element_type=F32)
    centered = values - per_channel[:1]
    square = jnp.broadcast_to(jnp.sum(centered * centered, axis=0, keepdims=True), (8, CH))
    spread_sq = jnp.dot(square, spread(CH, 128, False, GROUPS), precision=EXACT, preferred_element_type=F32)
    stat_ref[...] = jnp.broadcast_to((mean + spread_sq)[:1], stat_ref.shape)


def combine_stats(stats_ref, size):
    stats = stats_ref[...]
    devices = stats.shape[0]
    means = jnp.dot(stats, spread(128, CH, True, 0), precision=EXACT, preferred_element_type=F32)
    squares = jnp.dot(stats, spread(128, CH, True, GROUPS), precision=EXACT, preferred_element_type=F32)
    mean = jnp.sum(means, axis=0, keepdims=True) / devices
    away = means - mean
    total = jnp.sum(squares + size * (away * away), axis=0, keepdims=True)
    return mean, lax.rsqrt(total / (size * devices) + 1e-06)


def share_stats(stat):
    return lax.all_to_all(stat, ("frame", "height"), 0, 0, tiled=True)


def input_kernel(early_ref, behind_ref, own_ref, w_ref, bias_ref, base_ref, stat_ref):
    w = w_ref[...]
    lat = {}
    for k, ref in enumerate((early_ref, behind_ref, own_ref)):
        for i in range(FT):
            for r in range(RH + 6):
                value = ref[i, r].astype(F32)
                shifts = [value] + [pltpu.roll(value, 128 - e, 1) for e in (1, 2)]
                lat[k * FT + i, r] = jnp.concatenate([v.astype(BF16) for v in shifts], axis=0)
    for t in range(2 * FT):
        columns = []
        for r in range(RH + 4):
            columns.append(jnp.concatenate([lat[t + a, r + b] for a in range(3) for b in range(3)], axis=0))
        field = jnp.concatenate(columns, axis=1)
        total = lax.dot_general(field, w, TN, preferred_element_type=F32)
        total = (total + bias_ref[...]).astype(BF16).reshape(RH + 4, 128, CH)
        base_ref[t] = total[:, :WD]
    own = base_ref[FT:, 2 : RH + 2].reshape(CELLS, CH).astype(F32)
    local_stats(own, stat_ref)


def input_conv(latent, weight, bias, devices):
    return pl.pallas_call(
        input_kernel,
        in_specs=[VMEM] * 5,
        out_specs=[VMEM, VMEM],
        out_shape=[
            jax.ShapeDtypeStruct((2 * FT, RH + 4, WD, CH), BF16),
            jax.ShapeDtypeStruct((devices, 128), F32),
        ],
        compiler_params=pltpu.CompilerParams(vmem_limit_bytes=LIMIT),
        cost_estimate=pl.CostEstimate(flops=3 * 10**9, bytes_accessed=4 * 10**6, transcendentals=0),
        name="input_conv",
    )(*latent, weight, bias)


def after(value, earlier):
    return lax.optimization_barrier((value, earlier))[0]


CUT = 5


def quarter_kernel(one_ref, two_ref, place_ref, out_one, out_two, sems):
    copies = []
    for k in range(9):
        rows = pl.multiple_of(place_ref[3] * 16, 16)
        copies.append(pltpu.make_async_copy(one_ref.at[k % 3, :, k // 3, pl.ds(rows, 16)], out_one.at[k], sems.at[k]))
    for k in range(9 - CUT):
        rows = pl.multiple_of(place_ref[1] * 16, 16)
        source = two_ref.at[(CUT + k) % 3, :, (CUT + k) // 3, pl.ds(rows, 16)]
        copies.append(pltpu.make_async_copy(source, out_two.at[k], sems.at[9 + k]))
    for copy in copies:
        copy.start()
    for copy in copies:
        copy.wait()


def quarters_of(one, two, place):
    return pl.pallas_call(
        quarter_kernel,
        in_specs=[ANY, ANY, SMEM],
        out_specs=[VMEM] * 2,
        out_shape=[jax.ShapeDtypeStruct((n, 3, 16, CH), BF16) for n in (9, 9 - CUT)],
        scratch_shapes=[pltpu.SemaphoreType.DMA((18 - CUT,))],
        cost_estimate=pl.CostEstimate(flops=0, bytes_accessed=10**6, transcendentals=0),
        name="take_quarters",
    )(one, two, place)


def stack_kernel(*refs):
    *parts, out_ref, sems = refs
    copies = [pltpu.make_async_copy(part, out_ref.at[k], sems.at[k]) for k, part in enumerate(parts)]
    for copy in copies:
        copy.start()
    for copy in copies:
        copy.wait()


def stack(parts):
    return pl.pallas_call(
        stack_kernel,
        in_specs=[ANY] * len(parts),
        out_specs=VMEM,
        out_shape=jax.ShapeDtypeStruct((len(parts), *parts[0].shape), BF16),
        scratch_shapes=[pltpu.SemaphoreType.DMA((len(parts),))],
        compiler_params=pltpu.CompilerParams(vmem_limit_bytes=LIMIT),
        cost_estimate=pl.CostEstimate(flops=0, bytes_accessed=4 * 10**6, transcendentals=0),
        name="stack_parts",
    )(*parts)


def plane_groups():
    return [[(4 * y + x) * 8 + 2 * z + c for z in range(4) for x in range(4) for c in range(2)] for y in range(4)]


def plane_plan(array):
    return [
        (array, (8 * z + 2 * x + c, 3 * e), 0, 3, e, ("fixed", 2 * z + c, None, x))
        for e in range(3)
        for z in range(4)
        for x in range(4)
        for c in range(2)
    ]


def whole_plan(array):
    return [(array, k, k % 3, 1, k // 3, ("whole", 0, None, 0)) for k in range(CUT)]


def shard_plan(array, kind):
    return [(array, k // 3, k % 3, 1, k // 3, (kind, 0, None, 0)) for k in range(CUT, 9)]


Z_SHIFTS = (3, 1, 2)


def ring_plan(array, begin, end, kind, ring, step):
    plan = []
    k = begin
    while k < end:
        stop = min(end, k - k % 3 + 3)
        for i, z in enumerate(Z_SHIFTS):
            plan.append((array, (i, k - begin), k % 3, stop - k, k // 3, (kind, z, ring, step)))
        k = stop
    return plan


def conv_kernel(pieces, outs, height, products, taps, plan, weights, extras, *refs):
    refs = list(refs)
    raws = [refs.pop(0) for _ in pieces]
    stats_ref, flags_ref, place_ref, gain_ref, offset_ref = [refs.pop(0) for _ in range(5)]
    w_refs = [refs.pop(0) for _ in range(weights)]
    partial_ref = refs.pop(0) if "partial" in extras else None
    bias_ref = refs.pop(0) if "bias" in extras else None
    base_ref = refs.pop(0) if "base" in extras else None
    out_refs = [refs.pop(0) for _ in outs]
    stat_ref = refs.pop(0) if "stat" in extras else None
    field, wbuf, acc, sems = refs
    low, high = taps[0], taps[-1] + 1
    core, z = place_ref[0], place_ref[2]
    columns = sorted({copy[4] for copy in plan})
    for array, index, tap, length, e, (kind, shift, ring, step) in plan:
        slot = columns.index(e)
        begin, end = max(tap, low), min(tap + length, high)
        if begin >= end:
            continue
        taps_of = pl.ds(begin - low, end - begin)
        if kind == "whole":
            source, target = w_refs[array].at[pl.ds(index, 1)], wbuf.at[slot, taps_of]
        else:
            block = 2 * lax.rem(z + shift, 4) + (1 - core if kind == "other" else core)
            rows, width = block * 64, 16
            if kind == "fixed":
                rows = 64 * shift + 16 * step
            elif ring is None:
                width = 64
            else:
                rows = rows + lax.rem(place_ref[ring] + step, 4) * 16
            if kind != "fixed" and ring is None:
                source = w_refs[array].at[pl.ds(begin, end - begin), :, index]
            else:
                source = w_refs[array].at[index[0], pl.ds(index[1] + begin - tap, end - begin)]
            target = wbuf.at[slot, taps_of, :, pl.ds(pl.multiple_of(rows, 16), width)]
        pltpu.make_async_copy(source, target, sems.at[slot]).start()
    mean, inverse = combine_stats(stats_ref, CELLS * (CH // GROUPS))
    scale = inverse * gain_ref[...]
    offset = offset_ref[...]
    for raw, (frame, frames, row, rows, flag_of) in zip(raws, pieces):
        for i in frames:
            for j in range(rows):
                value = (raw[i, j].astype(F32) - mean) * scale + offset
                half = 0.5 * value
                value = half + half * jnp.tanh(half)
                for which in flag_of(i, j):
                    value = value * flags_ref[which]
                field[frame + i - frames[0], row + j, :WD] = value.astype(BF16)
                field[frame + i - frames[0], row + j, WD:] = jnp.zeros((WP - WD, CH), BF16)
    total = jnp.zeros((len(outs) * height * WP, CH), F32)
    edge = jnp.zeros((1, CH), F32)
    for e, column in enumerate(columns):
        pltpu.make_async_copy(wbuf.at[e], wbuf.at[e], sems.at[e]).wait()
        for n, t in enumerate(outs):
            terms = [(f, a) for (out, f, a) in products if out == t]
            xs = [field[f, b : b + height].reshape(height * WP, CH) for f, a in terms for b in range(3)]
            ws = [wbuf[e, a - low, b] for f, a in terms for b in range(3)]
            acc[e, pl.ds(n * height * WP, height * WP)] = lax.dot_general(
                jnp.concatenate(xs, axis=1), jnp.concatenate(ws, axis=1), NT, preferred_element_type=F32
            )
    for e, column in enumerate(columns):
        if column == 0:
            total = total + jnp.concatenate([edge, acc[e, :-1]], axis=0)
        elif column == 1:
            total = total + acc[e]
        else:
            total = total + jnp.concatenate([acc[e, 1:], edge], axis=0)
    total = total.reshape(len(outs), height, WP, CH)[:, :, :WD]
    span = pl.ds(outs[0], len(outs))
    if partial_ref is not None:
        total = total + partial_ref[span]
    if bias_ref is not None:
        total = total + bias_ref[...]
    if base_ref is not None:
        total = total + base_ref[pl.ds(FT + outs[0], len(outs)), 2 : RH + 2].astype(F32)
    for n, out_ref in enumerate(out_refs):
        out_ref[...] = total[n : n + 1].astype(out_ref.dtype)
    if stat_ref is not None:
        own = total[:, 1 : RH + 1].astype(BF16).astype(F32)
        local_stats(own.reshape(CELLS, CH), stat_ref)


def block_conv(name, raws, pieces, outs, height, products, stats, flags, place, gain, offset, weight, extras, kind, devices):
    arrays, plan = weight
    columns = len({copy[4] for copy in plan})
    taps = sorted({a for _, _, a in products})
    frames = max(f for _, f, _ in products) + 1
    args = [*raws, stats, flags, place, gain, offset, *arrays]
    args += [extras[k] for k in ("partial", "bias", "base") if k in extras]
    specs = [*[VMEM] * len(raws), VMEM, SMEM, SMEM, VMEM, VMEM, *[ANY] * len(arrays)]
    specs += [VMEM] * (len(args) - len(specs))
    shapes = [jax.ShapeDtypeStruct((1, height, WD, CH), kind)] * len(outs)
    if "stat" in extras:
        shapes.append(jax.ShapeDtypeStruct((devices, 128), F32))
    return pl.pallas_call(
        functools.partial(conv_kernel, pieces, outs, height, products, taps, plan, len(arrays), tuple(extras)),
        in_specs=specs,
        out_specs=[VMEM] * len(shapes),
        out_shape=shapes,
        scratch_shapes=[
            pltpu.VMEM((frames, height + 2, WP, CH), BF16),
            pltpu.VMEM((columns, len(taps), 3, CH, CH), BF16),
            pltpu.VMEM((columns, len(outs) * height * WP, CH), F32),
            pltpu.SemaphoreType.DMA((columns,)),
        ],
        compiler_params=pltpu.CompilerParams(vmem_limit_bytes=LIMIT),
        cost_estimate=pl.CostEstimate(
            flops=len(products) * 2 * 3 * columns * height * WP * CH * CH, bytes_accessed=16 * 10**6, transcendentals=0
        ),
        name=name,
    )(*args)


def upsample_kernel(*refs):
    first, second, third, w_ref, bias_ref = refs[:5]
    out_ref, field = refs[-2:]

    @pl.when(pl.program_id(0) == 0)
    def _():
        for k, ref in enumerate((first, second, third)):
            for r in range(RH):
                field[k, r, :WD] = ref[0, r]
                field[k, r, WD:] = jnp.zeros((WP - WD, CH), BF16)

    parts = jnp.concatenate([field[k].reshape(RH * WP, CH) for k in range(3)], axis=1)
    total = jnp.dot(parts, w_ref[...].reshape(3 * CH, CH), preferred_element_type=F32) + bias_ref[...]
    total = total.astype(BF16).reshape(RH, WP, CH)
    twice = lax.broadcasted_iota(jnp.int32, (2 * WD, WP), 0) // 2 == lax.broadcasted_iota(jnp.int32, (2 * WD, WP), 1)
    twice = twice.astype(F32).astype(BF16)
    for r in range(RH):
        wide = jnp.dot(twice, total[r], preferred_element_type=F32).astype(BF16)
        out_ref[0, 2 * r] = wide
        out_ref[0, 2 * r + 1] = wide


def upsample(t, frames, weight, bias, out):
    frame = pl.BlockSpec((1, RH, WD, CH), lambda s: (0, 0, 0, 0))
    return pl.pallas_call(
        upsample_kernel,
        grid=(2,),
        in_specs=[
            frame,
            frame,
            frame,
            pl.BlockSpec((3, CH, CH), lambda s: (0, 0, s)),
            pl.BlockSpec((1, CH), lambda s: (0, s)),
            *([] if out is None else [ANY]),
        ],
        out_specs=pl.BlockSpec((1, 2 * RH, 2 * WD, CH), lambda s: (2 * t + s, 0, 0, 0)),
        out_shape=jax.ShapeDtypeStruct((2 * FT, 2 * RH, 2 * WD, CH), BF16),
        scratch_shapes=[pltpu.VMEM((3, RH, WP, CH), BF16)],
        input_output_aliases={} if out is None else {5: 0},
        compiler_params=pltpu.CompilerParams(vmem_limit_bytes=LIMIT),
        cost_estimate=pl.CostEstimate(flops=15 * 10**8, bytes_accessed=6 * 10**6, transcendentals=0),
        name="upsample",
    )(*frames, weight, bias, *([] if out is None else [out]))


def deal_kernel(tokens_ref, line_ref, column_ref, tile_ref, tile_down_ref, out_ref):
    tiles = out_ref.shape[0]
    count = tokens_ref.shape[1]
    tile = tile_ref[...]
    same = tile_down_ref[...] == tile
    earlier = lax.broadcasted_iota(jnp.int32, (count, count), 0) < lax.broadcasted_iota(jnp.int32, (count, count), 1)
    rank = jnp.sum((same & earlier).astype(F32), axis=0, keepdims=True)
    slot = tile * 128 + rank.astype(jnp.int32)
    onto = lax.broadcasted_iota(jnp.int32, (tiles * 128, count), 0) == slot
    rest = jnp.zeros((14, count), F32)
    value = [tokens_ref[...].astype(F32), line_ref[...].astype(F32), column_ref[...].astype(F32), rest]
    value = jnp.concatenate(value, axis=0).astype(BF16)
    dealt = lax.dot_general(value, onto.astype(F32).astype(BF16), NT, preferred_element_type=F32).astype(BF16)
    for g in range(tiles):
        for k in range(3):
            near = g + k - 1
            if 0 <= near < tiles:
                out_ref[g, k] = dealt[:, near * 128 : near * 128 + 128]
            else:
                out_ref[g, k] = jnp.zeros((32, 128), BF16)


def place_kernel(dealt_ref, first_ref, out_ref):
    blocks = [dealt_ref[i, k].astype(F32) for i in range(dealt_ref.shape[0]) for k in range(3)]
    dealt = jnp.concatenate(blocks, axis=1)
    value, line, column = dealt[:ZC], dealt[ZC : ZC + 1], dealt[ZC + 1 : ZC + 2]
    count = dealt.shape[1]
    first = first_ref[0]
    field = []
    for t in range(FT):
        for i in range(RH + 6):
            row = first + i
            wanted = jnp.where((row >= 0) & (row < 32), t * 32 + row, -1).astype(F32)
            field.append(jnp.where(line == wanted, value, 0.0))
    onto = lax.broadcasted_iota(jnp.int32, (128, count), 0).astype(F32) == column
    placed = lax.dot_general(
        jnp.concatenate(field, axis=0).astype(BF16), onto.astype(F32).astype(BF16), NT, preferred_element_type=F32
    )
    out_ref[...] = placed.astype(BF16).reshape(out_ref.shape)


def latent_own(tokens, token_pos):
    tiles = lax.axis_size("height")
    mine = lax.axis_index("height")
    count = tokens.shape[1]
    places = lax.dynamic_slice_in_dim(token_pos, mine * count, count, 0)
    line = places // WD - lax.axis_index("frame") * (FT * RH * tiles)
    column = places % WD + 1
    tile = line % (RH * tiles) // RH
    params = pltpu.CompilerParams(vmem_limit_bytes=LIMIT)
    cost = pl.CostEstimate(flops=3 * 10**8, bytes_accessed=10**6, transcendentals=0)
    across = lambda v: v.reshape(1, count)
    dealt = pl.pallas_call(
        deal_kernel,
        in_specs=[VMEM] * 5,
        out_specs=VMEM,
        out_shape=jax.ShapeDtypeStruct((tiles, 3, 32, 128), BF16),
        compiler_params=params,
        cost_estimate=cost,
        name="deal_tokens",
    )(tokens, across(line), across(column), across(tile), tile.reshape(count, 1))
    dealt = lax.all_to_all(dealt, "height", 0, 0, tiled=True)
    return pl.pallas_call(
        place_kernel,
        in_specs=[VMEM, SMEM],
        out_specs=VMEM,
        out_shape=jax.ShapeDtypeStruct((FT, RH + 6, ZC, 128), BF16),
        compiler_params=params,
        cost_estimate=cost,
        name="place_tokens",
    )(dealt, (mine * RH - 3).reshape(1).astype(jnp.int32))


def latent_slabs(own):
    return along(own, "frame", 2), along(own, "frame", 1), own


def on_device(
    tokens,
    token_pos,
    weight_in,
    bias_in,
    gain_one,
    offset_one,
    weight_one,
    bias_one,
    gain_two,
    offset_two,
    weight_two,
    bias_two,
    weight_time,
    bias_time,
):
    devices = lax.axis_size("frame") * lax.axis_size("height")
    slab, tile = lax.axis_index("frame"), lax.axis_index("height")
    place = jnp.stack([tile % 2, slab // 4, tile // 2, slab % 4]).astype(jnp.int32)
    flags = jnp.stack([slab > 0, tile > 0, tile < lax.axis_size("height") - 1]).astype(F32)
    row = lambda v: v.reshape(1, -1)

    def send_y(v, k):
        return lax.ppermute(v, "frame", [(4 * y + x, 4 * ((y + k) % 4) + x) for y in range(4) for x in range(4)])

    def swap_core(v):
        return lax.ppermute(v, "height", [(i, i ^ 1) for i in range(8)])

    def send_z(v, k):
        return lax.ppermute(v, "height", [(i, (i + 2 * k) % 8) for i in range(8)])

    shard_one, shard_two = jnp.swapaxes(weight_one, 3, 4), jnp.swapaxes(weight_two, 3, 4)
    quarter_one, quarter_two = quarters_of(shard_one, shard_two, place)
    one = lax.all_gather(quarter_one, ("frame", "height"), axis_index_groups=plane_groups())
    sent = [send_z(quarter_two, k) for k in (1, 3, 2)]
    own = latent_own(after(tokens, quarter_one), token_pos)
    latent = latent_slabs(own)
    near = stack([after(v, latent[0]) for v in sent])
    held = [send_y(near, k) if k else near for k in (0, 1, -1, 2)]
    base, stat = input_conv([after(v, near) for v in latent], weight_in.reshape(-1, CH), row(bias_in), devices)
    shared = share_stats(stat)
    taps_two = jnp.transpose(after(shard_two, base), (2, 0, 1, 3, 4)).reshape(9, 3, -1, CH)[:CUT]
    two = lax.all_gather(taps_two, "height", axis=2, tiled=True)
    swapped = [swap_core(v) for v in held]

    def rows(beyond):
        return lambda i, j: [1] if j < beyond else [2] if j >= RH + beyond else []

    everything = lambda i, j: ([0] if i < FT else []) + rows(2)(i, j)
    norm_one = (shared, flags, place, row(gain_one), row(offset_one))
    common = ([after(base, tuple(held))], [(0, range(2 * FT), 0, RH + 4, everything)], [0, 1], RH + 2, [(t, t + a, a) for t in range(FT) for a in range(3)])
    *inner, stat = block_conv(
        "conv_one",
        *common,
        *norm_one,
        ([one], plane_plan(0)),
        {"bias": row(bias_one), "stat": None},
        BF16,
        devices,
    )
    shared = share_stats(stat)
    behind = [along(after(inner[0], shared), "frame", 1), along(inner[1], "frame", 1)]
    plan = whole_plan(0) + shard_plan(1, "own") + shard_plan(2, "other")
    for k, step in enumerate((0, 3, 1, 2)):
        plan += ring_plan(3 + k, CUT, 9, "own", 1, step) + ring_plan(7 + k, CUT, 9, "other", 1, step)
    kernel_two = ([two, shard_two, swap_core(after(shard_two, base)), *held, *swapped], plan)
    norm_two = (shared, flags, place, row(gain_two), row(offset_two))

    hidden = lambda i, j: [0] + rows(1)(i, j)
    extras = {"bias": row(bias_two), "base": base}
    (late,) = block_conv(
        "conv_two_late",
        [behind[1], *inner],
        [(k, range(1), 0, RH + 2, rows(1) if k else hidden) for k in range(3)],
        [1],
        RH,
        [(1, a, a) for a in range(3)],
        *norm_two,
        kernel_two,
        extras,
        BF16,
        devices,
    )
    late_halo = along(late, "frame", 1)
    (early,) = block_conv(
        "conv_two_early",
        [*behind, after(inner[0], late)],
        [(k, range(1), 0, RH + 2, hidden if k < FT else rows(1)) for k in range(3)],
        [0],
        RH,
        [(0, a, a) for a in range(3)],
        *norm_two,
        kernel_two,
        extras,
        BF16,
        devices,
    )
    early_halo = along(early, "frame", 1)
    out = upsample(1, [late_halo, early, late], weight_time, row(bias_time), None)
    return upsample(0, [early_halo, late_halo, early], weight_time, row(bias_time), out)


def solution(mesh):
    placed = (
        P(None, ("frame", "height")),
        P("frame"),
        P(),
        P(),
        P(),
        P(),
        P(None, None, None, None, "height"),
        P(),
        P(),
        P(),
        P(None, None, None, None, "height"),
        P(),
        P(),
        P(),
    )
    return jax.shard_map(
        on_device,
        mesh=mesh,
        in_specs=placed,
        out_specs=P("frame", "height", None, None),
        check_vma=False,
    )
```

```python
import functools

import jax
import jax.numpy as jnp
from jax import lax
from jax.experimental import pallas as pl
from jax.experimental.pallas import tpu as pltpu
from jax.sharding import PartitionSpec as P

GROUPS = 32
ZC = 16
FT = 2
RH = 4
WD = 104
WP = 112
CH = 512
CELLS = FT * RH * WD
F32 = jnp.float32
BF16 = jnp.bfloat16
NT = (((1,), (1,)), ((), ()))
TN = (((0,), (0,)), ((), ()))
VMEM = pl.BlockSpec(memory_space=pltpu.VMEM)
SMEM = pl.BlockSpec(memory_space=pltpu.SMEM)
ANY = pl.BlockSpec(memory_space=pl.ANY)
EXACT = lax.Precision.HIGHEST
LIMIT = 44 * 2**20


def along(value, axis, steps):
    count = lax.axis_size(axis)
    leading, last = (max(0, -steps), min(count, count - steps))
    return lax.ppermute(value, axis, [(source, source + steps) for source in range(leading, last)])


def spread(rows, cols, lanes_first, shift):
    one = lax.broadcasted_iota(jnp.int32, (rows, cols), 0)
    two = lax.broadcasted_iota(jnp.int32, (rows, cols), 1)
    lane, channel = (one, two) if lanes_first else (two, one)
    return (lane == channel // (CH // GROUPS) + shift).astype(F32)


def local_stats(values, stat_ref):
    cells = values.shape[0]
    total = jnp.broadcast_to(jnp.sum(values, axis=0, keepdims=True), (8, CH))
    size = cells * (CH // GROUPS)
    mean = jnp.dot(total, spread(CH, 128, False, 0), precision=EXACT, preferred_element_type=F32) / size
    per_channel = jnp.dot(mean, spread(128, CH, True, 0), precision=EXACT, preferred_element_type=F32)
    centered = values - per_channel[:1]
    square = jnp.broadcast_to(jnp.sum(centered * centered, axis=0, keepdims=True), (8, CH))
    spread_sq = jnp.dot(square, spread(CH, 128, False, GROUPS), precision=EXACT, preferred_element_type=F32)
    stat_ref[...] = jnp.broadcast_to((mean + spread_sq)[:1], stat_ref.shape)


def combine_stats(stats_ref, size):
    stats = stats_ref[...]
    devices = stats.shape[0]
    means = jnp.dot(stats, spread(128, CH, True, 0), precision=EXACT, preferred_element_type=F32)
    squares = jnp.dot(stats, spread(128, CH, True, GROUPS), precision=EXACT, preferred_element_type=F32)
    mean = jnp.sum(means, axis=0, keepdims=True) / devices
    away = means - mean
    total = jnp.sum(squares + size * (away * away), axis=0, keepdims=True)
    return mean, lax.rsqrt(total / (size * devices) + 1e-06)


def share_stats(stat):
    return lax.all_to_all(stat, ("frame", "height"), 0, 0, tiled=True)


def input_kernel(early_ref, behind_ref, own_ref, w_ref, bias_ref, base_ref, stat_ref):
    w = w_ref[...]
    lat = {}
    for k, ref in enumerate((early_ref, behind_ref, own_ref)):
        for i in range(FT):
            for r in range(RH + 6):
                value = ref[i, r].astype(F32)
                shifts = [value] + [pltpu.roll(value, 128 - e, 1) for e in (1, 2)]
                lat[k * FT + i, r] = jnp.concatenate([v.astype(BF16) for v in shifts], axis=0)
    for t in range(2 * FT):
        columns = []
        for r in range(RH + 4):
            columns.append(jnp.concatenate([lat[t + a, r + b] for a in range(3) for b in range(3)], axis=0))
        field = jnp.concatenate(columns, axis=1)
        total = lax.dot_general(field, w, TN, preferred_element_type=F32)
        total = (total + bias_ref[...]).astype(BF16).reshape(RH + 4, 128, CH)
        base_ref[t] = total[:, :WD]
    own = base_ref[FT:, 2 : RH + 2].reshape(CELLS, CH).astype(F32)
    local_stats(own, stat_ref)


def input_conv(latent, weight, bias, devices):
    return pl.pallas_call(
        input_kernel,
        in_specs=[VMEM] * 5,
        out_specs=[VMEM, VMEM],
        out_shape=[
            jax.ShapeDtypeStruct((2 * FT, RH + 4, WD, CH), BF16),
            jax.ShapeDtypeStruct((devices, 128), F32),
        ],
        compiler_params=pltpu.CompilerParams(vmem_limit_bytes=LIMIT),
        cost_estimate=pl.CostEstimate(flops=3 * 10**9, bytes_accessed=4 * 10**6, transcendentals=0),
        name="input_conv",
    )(*latent, weight, bias)


def after(value, earlier):
    return lax.optimization_barrier((value, earlier))[0]


CUT = 5


def quarter_kernel(w_ref, place_ref, out_ref, sems):
    copies = []
    for k in range(9 - CUT):
        rows = pl.multiple_of(place_ref[1] * 16, 16)
        source = w_ref.at[(CUT + k) % 3, :, (CUT + k) // 3, pl.ds(rows, 16)]
        copies.append(pltpu.make_async_copy(source, out_ref.at[k], sems.at[k]))
    for copy in copies:
        copy.start()
    for copy in copies:
        copy.wait()


def quarter_of(weight, place):
    return pl.pallas_call(
        quarter_kernel,
        in_specs=[ANY, SMEM],
        out_specs=VMEM,
        out_shape=jax.ShapeDtypeStruct((9 - CUT, 3, 16, CH), BF16),
        scratch_shapes=[pltpu.SemaphoreType.DMA((9 - CUT,))],
        cost_estimate=pl.CostEstimate(flops=0, bytes_accessed=10**6, transcendentals=0),
        name="take_quarter",
    )(weight, place)


def stack_kernel(*refs):
    *parts, out_ref, sems = refs
    copies = [pltpu.make_async_copy(part, out_ref.at[k], sems.at[k]) for k, part in enumerate(parts)]
    for copy in copies:
        copy.start()
    for copy in copies:
        copy.wait()


def stack(parts):
    return pl.pallas_call(
        stack_kernel,
        in_specs=[ANY] * len(parts),
        out_specs=VMEM,
        out_shape=jax.ShapeDtypeStruct((len(parts), *parts[0].shape), BF16),
        scratch_shapes=[pltpu.SemaphoreType.DMA((len(parts),))],
        compiler_params=pltpu.CompilerParams(vmem_limit_bytes=LIMIT),
        cost_estimate=pl.CostEstimate(flops=0, bytes_accessed=4 * 10**6, transcendentals=0),
        name="stack_parts",
    )(*parts)


def plane_groups():
    return [[(4 * y + x) * 8 + 2 * z + c for z in range(4) for x in range(4) for c in range(2)] for y in range(4)]


def plane_plan(array):
    return [
        (array, 8 * z + 2 * x + c, 0, 3, e, ("fixed", 2 * z + c, None, x))
        for e in range(3)
        for z in range(4)
        for x in range(4)
        for c in range(2)
    ]


def whole_plan(array):
    return [(array, k, k % 3, 1, k // 3, ("whole", 0, None, 0)) for k in range(CUT)]


def shard_plan(array, kind):
    return [(array, k // 3, k % 3, 1, k // 3, (kind, 0, None, 0)) for k in range(CUT, 9)]


Z_SHIFTS = (3, 1, 2)


def ring_plan(array, begin, end, kind, ring, step):
    plan = []
    k = begin
    while k < end:
        stop = min(end, k - k % 3 + 3)
        for i, z in enumerate(Z_SHIFTS):
            plan.append((array, (i, k - begin), k % 3, stop - k, k // 3, (kind, z, ring, step)))
        k = stop
    return plan


def conv_kernel(pieces, outs, height, products, taps, plan, weights, extras, *refs):
    refs = list(refs)
    raws = [refs.pop(0) for _ in pieces]
    stats_ref, flags_ref, place_ref, gain_ref, offset_ref = [refs.pop(0) for _ in range(5)]
    w_refs = [refs.pop(0) for _ in range(weights)]
    partial_ref = refs.pop(0) if "partial" in extras else None
    bias_ref = refs.pop(0) if "bias" in extras else None
    base_ref = refs.pop(0) if "base" in extras else None
    out_refs = [refs.pop(0) for _ in outs]
    stat_ref = refs.pop(0) if "stat" in extras else None
    field, wbuf, acc, sems = refs
    low, high = taps[0], taps[-1] + 1
    core, z = place_ref[0], place_ref[2]
    columns = sorted({copy[4] for copy in plan})
    copies = [[] for _ in columns]
    for array, index, tap, length, e, (kind, shift, ring, step) in plan:
        slot = columns.index(e)
        begin, end = max(tap, low), min(tap + length, high)
        if begin >= end:
            continue
        taps_of = pl.ds(begin - low, end - begin)
        if kind == "whole":
            source, target = w_refs[array].at[pl.ds(index, 1)], wbuf.at[slot, taps_of]
        else:
            block = 2 * lax.rem(z + shift, 4) + (1 - core if kind == "other" else core)
            rows, width = block * 64, 16
            if kind == "fixed":
                rows = 64 * shift + 16 * step
            elif ring is None:
                width = 64
            else:
                rows = rows + lax.rem(place_ref[ring] + step, 4) * 16
            if kind == "fixed":
                source = w_refs[array].at[index, pl.ds(begin, end - begin), :, e]
            elif ring is None:
                source = w_refs[array].at[pl.ds(begin, end - begin), :, index]
            else:
                source = w_refs[array].at[index[0], pl.ds(index[1] + begin - tap, end - begin)]
            target = wbuf.at[slot, taps_of, :, pl.ds(pl.multiple_of(rows, 16), width)]
        copies[slot].append(pltpu.make_async_copy(source, target, sems.at[slot]))
    for copy in copies[0]:
        copy.start()
    mean, inverse = combine_stats(stats_ref, CELLS * (CH // GROUPS))
    scale = inverse * gain_ref[...]
    offset = offset_ref[...]
    for raw, (frame, frames, row, rows, flag_of) in zip(raws, pieces):
        for i in frames:
            for j in range(rows):
                value = (raw[i, j].astype(F32) - mean) * scale + offset
                half = 0.5 * value
                value = half + half * jnp.tanh(half)
                for which in flag_of(i, j):
                    value = value * flags_ref[which]
                field[frame + i - frames[0], row + j, :WD] = value.astype(BF16)
                field[frame + i - frames[0], row + j, WD:] = jnp.zeros((WP - WD, CH), BF16)
    for later in copies[1:]:
        for copy in later:
            copy.start()
    total = jnp.zeros((len(outs) * height * WP, CH), F32)
    edge = jnp.zeros((1, CH), F32)
    for e, column in enumerate(columns):
        pltpu.make_async_copy(wbuf.at[e], wbuf.at[e], sems.at[e]).wait()
        for n, t in enumerate(outs):
            terms = [(f, a) for (out, f, a) in products if out == t]
            xs = [field[f, b : b + height].reshape(height * WP, CH) for f, a in terms for b in range(3)]
            ws = [wbuf[e, a - low, b] for f, a in terms for b in range(3)]
            acc[e, pl.ds(n * height * WP, height * WP)] = lax.dot_general(
                jnp.concatenate(xs, axis=1), jnp.concatenate(ws, axis=1), NT, preferred_element_type=F32
            )
    for e, column in enumerate(columns):
        if column == 0:
            total = total + jnp.concatenate([edge, acc[e, :-1]], axis=0)
        elif column == 1:
            total = total + acc[e]
        else:
            total = total + jnp.concatenate([acc[e, 1:], edge], axis=0)
    total = total.reshape(len(outs), height, WP, CH)[:, :, :WD]
    span = pl.ds(outs[0], len(outs))
    if partial_ref is not None:
        total = total + partial_ref[span]
    if bias_ref is not None:
        total = total + bias_ref[...]
    if base_ref is not None:
        total = total + base_ref[pl.ds(FT + outs[0], len(outs)), 2 : RH + 2].astype(F32)
    for n, out_ref in enumerate(out_refs):
        out_ref[...] = total[n : n + 1].astype(out_ref.dtype)
    if stat_ref is not None:
        own = total[:, 1 : RH + 1].astype(BF16).astype(F32)
        local_stats(own.reshape(CELLS, CH), stat_ref)


def block_conv(name, raws, pieces, outs, height, products, stats, flags, place, gain, offset, weight, extras, kind, devices):
    arrays, plan = weight
    columns = len({copy[4] for copy in plan})
    taps = sorted({a for _, _, a in products})
    frames = max(f for _, f, _ in products) + 1
    args = [*raws, stats, flags, place, gain, offset, *arrays]
    args += [extras[k] for k in ("partial", "bias", "base") if k in extras]
    specs = [*[VMEM] * len(raws), VMEM, SMEM, SMEM, VMEM, VMEM, *[ANY] * len(arrays)]
    specs += [VMEM] * (len(args) - len(specs))
    shapes = [jax.ShapeDtypeStruct((1, height, WD, CH), kind)] * len(outs)
    if "stat" in extras:
        shapes.append(jax.ShapeDtypeStruct((devices, 128), F32))
    return pl.pallas_call(
        functools.partial(conv_kernel, pieces, outs, height, products, taps, plan, len(arrays), tuple(extras)),
        in_specs=specs,
        out_specs=[VMEM] * len(shapes),
        out_shape=shapes,
        scratch_shapes=[
            pltpu.VMEM((frames, height + 2, WP, CH), BF16),
            pltpu.VMEM((columns, len(taps), 3, CH, CH), BF16),
            pltpu.VMEM((columns, len(outs) * height * WP, CH), F32),
            pltpu.SemaphoreType.DMA((columns,)),
        ],
        compiler_params=pltpu.CompilerParams(vmem_limit_bytes=LIMIT if "stat" in extras else 60 * 2**20),
        cost_estimate=pl.CostEstimate(
            flops=len(products) * 2 * 3 * columns * height * WP * CH * CH, bytes_accessed=16 * 10**6, transcendentals=0
        ),
        name=name,
    )(*args)


def upsample_kernel(*refs):
    first, second, third, w_ref, bias_ref = refs[:5]
    out_ref, field = refs[-2:]

    @pl.when(pl.program_id(0) == 0)
    def _():
        for k, ref in enumerate((first, second, third)):
            for r in range(RH):
                field[k, r, :WD] = ref[0, r]
                field[k, r, WD:] = jnp.zeros((WP - WD, CH), BF16)

    parts = jnp.concatenate([field[k].reshape(RH * WP, CH) for k in range(3)], axis=1)
    total = jnp.dot(parts, w_ref[...].reshape(3 * CH, CH // 2), preferred_element_type=F32) + bias_ref[...]
    total = total.astype(BF16).reshape(RH, WP, CH // 2)
    twice = lax.broadcasted_iota(jnp.int32, (2 * WD, WP), 0) // 2 == lax.broadcasted_iota(jnp.int32, (2 * WD, WP), 1)
    twice = twice.astype(F32).astype(BF16)
    for r in range(RH):
        wide = jnp.dot(twice, total[r], preferred_element_type=F32).astype(BF16)
        out_ref[0, 2 * r] = wide
        out_ref[0, 2 * r + 1] = wide


def upsample(t, frames, weight, bias, out):
    frame = pl.BlockSpec((1, RH, WD, CH), lambda s: (0, 0, 0, 0))
    return pl.pallas_call(
        upsample_kernel,
        grid=(4,),
        in_specs=[
            frame,
            frame,
            frame,
            pl.BlockSpec((3, CH, CH // 2), lambda s: (0, 0, s)),
            pl.BlockSpec((1, CH // 2), lambda s: (0, s)),
            *([] if out is None else [ANY]),
        ],
        out_specs=pl.BlockSpec((1, 2 * RH, 2 * WD, CH // 2), lambda s: (2 * t + s // 2, 0, 0, s % 2)),
        out_shape=jax.ShapeDtypeStruct((2 * FT, 2 * RH, 2 * WD, CH), BF16),
        scratch_shapes=[pltpu.VMEM((3, RH, WP, CH), BF16)],
        input_output_aliases={} if out is None else {5: 0},
        compiler_params=pltpu.CompilerParams(vmem_limit_bytes=LIMIT),
        cost_estimate=pl.CostEstimate(flops=15 * 10**8, bytes_accessed=6 * 10**6, transcendentals=0),
        name="upsample",
    )(*frames, weight, bias, *([] if out is None else [out]))


def deal_kernel(tokens_ref, line_ref, column_ref, tile_ref, tile_down_ref, out_ref):
    tiles = out_ref.shape[0]
    count = tokens_ref.shape[1]
    tile = tile_ref[...]
    same = tile_down_ref[...] == tile
    earlier = lax.broadcasted_iota(jnp.int32, (count, count), 0) < lax.broadcasted_iota(jnp.int32, (count, count), 1)
    rank = jnp.sum((same & earlier).astype(F32), axis=0, keepdims=True)
    slot = tile * 128 + rank.astype(jnp.int32)
    onto = lax.broadcasted_iota(jnp.int32, (tiles * 128, count), 0) == slot
    rest = jnp.zeros((14, count), F32)
    value = [tokens_ref[...].astype(F32), line_ref[...].astype(F32), column_ref[...].astype(F32), rest]
    value = jnp.concatenate(value, axis=0).astype(BF16)
    dealt = lax.dot_general(value, onto.astype(F32).astype(BF16), NT, preferred_element_type=F32).astype(BF16)
    for g in range(tiles):
        for k in range(3):
            near = g + k - 1
            if 0 <= near < tiles:
                out_ref[g, k] = dealt[:, near * 128 : near * 128 + 128]
            else:
                out_ref[g, k] = jnp.zeros((32, 128), BF16)


def place_kernel(dealt_ref, first_ref, out_ref):
    blocks = [dealt_ref[i, k].astype(F32) for i in range(dealt_ref.shape[0]) for k in range(3)]
    dealt = jnp.concatenate(blocks, axis=1)
    value, line, column = dealt[:ZC], dealt[ZC : ZC + 1], dealt[ZC + 1 : ZC + 2]
    count = dealt.shape[1]
    first = first_ref[0]
    field = []
    for t in range(FT):
        for i in range(RH + 6):
            row = first + i
            wanted = jnp.where((row >= 0) & (row < 32), t * 32 + row, -1).astype(F32)
            field.append(jnp.where(line == wanted, value, 0.0))
    onto = lax.broadcasted_iota(jnp.int32, (128, count), 0).astype(F32) == column
    placed = lax.dot_general(
        jnp.concatenate(field, axis=0).astype(BF16), onto.astype(F32).astype(BF16), NT, preferred_element_type=F32
    )
    out_ref[...] = placed.astype(BF16).reshape(out_ref.shape)


def latent_own(tokens, token_pos):
    tiles = lax.axis_size("height")
    mine = lax.axis_index("height")
    count = tokens.shape[1]
    places = lax.dynamic_slice_in_dim(token_pos, mine * count, count, 0)
    line = places // WD - lax.axis_index("frame") * (FT * RH * tiles)
    column = places % WD + 1
    tile = line % (RH * tiles) // RH
    params = pltpu.CompilerParams(vmem_limit_bytes=LIMIT)
    cost = pl.CostEstimate(flops=3 * 10**8, bytes_accessed=10**6, transcendentals=0)
    across = lambda v: v.reshape(1, count)
    dealt = pl.pallas_call(
        deal_kernel,
        in_specs=[VMEM] * 5,
        out_specs=VMEM,
        out_shape=jax.ShapeDtypeStruct((tiles, 3, 32, 128), BF16),
        compiler_params=params,
        cost_estimate=cost,
        name="deal_tokens",
    )(tokens, across(line), across(column), across(tile), tile.reshape(count, 1))
    dealt = lax.all_to_all(dealt, "height", 0, 0, tiled=True)
    return pl.pallas_call(
        place_kernel,
        in_specs=[VMEM, SMEM],
        out_specs=VMEM,
        out_shape=jax.ShapeDtypeStruct((FT, RH + 6, ZC, 128), BF16),
        compiler_params=params,
        cost_estimate=cost,
        name="place_tokens",
    )(dealt, (mine * RH - 3).reshape(1).astype(jnp.int32))


def latent_slabs(own):
    return along(own, "frame", 2), along(own, "frame", 1), own


def on_device(
    tokens,
    token_pos,
    weight_in,
    bias_in,
    gain_one,
    offset_one,
    weight_one,
    bias_one,
    gain_two,
    offset_two,
    weight_two,
    bias_two,
    weight_time,
    bias_time,
):
    devices = lax.axis_size("frame") * lax.axis_size("height")
    slab, tile = lax.axis_index("frame"), lax.axis_index("height")
    place = jnp.stack([tile % 2, slab // 4, tile // 2, slab % 4]).astype(jnp.int32)
    flags = jnp.stack([slab > 0, tile > 0, tile < lax.axis_size("height") - 1]).astype(F32)
    row = lambda v: v.reshape(1, -1)

    def send_y(v, k):
        return lax.ppermute(v, "frame", [(4 * y + x, 4 * ((y + k) % 4) + x) for y in range(4) for x in range(4)])

    def swap_core(v):
        return lax.ppermute(v, "height", [(i, i ^ 1) for i in range(8)])

    def send_z(v, k):
        return lax.ppermute(v, "height", [(i, (i + 2 * k) % 8) for i in range(8)])

    shard_one, shard_two = jnp.swapaxes(weight_one, 3, 4), jnp.swapaxes(weight_two, 3, 4)
    quarter_one = lax.dynamic_slice(shard_one, (0, 0, 0, 16 * (slab % 4), 0), (3, 3, 3, 16, CH))
    quarter_two = quarter_of(after(shard_two, quarter_one), place)
    one = lax.all_gather(quarter_one, ("frame", "height"), axis_index_groups=plane_groups())
    sent = [send_z(quarter_two, k) for k in (1, 3, 2)]
    own = latent_own(after(tokens, quarter_one), token_pos)
    latent = latent_slabs(own)
    near = stack([after(v, latent[0]) for v in sent])
    held = [send_y(near, k) if k else near for k in (0, 1, -1, 2)]
    base, stat = input_conv([after(v, near) for v in latent], weight_in.reshape(-1, CH), row(bias_in), devices)
    shared = share_stats(stat)
    taps_two = jnp.transpose(after(shard_two, base), (2, 0, 1, 3, 4)).reshape(9, 3, -1, CH)[:CUT]
    two = lax.all_gather(taps_two, "height", axis=2, tiled=True)
    swapped = [swap_core(v) for v in held]

    def rows(beyond):
        return lambda i, j: [1] if j < beyond else [2] if j >= RH + beyond else []

    everything = lambda i, j: ([0] if i < FT else []) + rows(2)(i, j)
    norm_one = (shared, flags, place, row(gain_one), row(offset_one))
    common = ([after(base, tuple(held))], [(0, range(2 * FT), 0, RH + 4, everything)], [0, 1], RH + 2, [(t, t + a, a) for t in range(FT) for a in range(3)])
    *inner, stat = block_conv(
        "conv_one",
        *common,
        *norm_one,
        ([one], plane_plan(0)),
        {"bias": row(bias_one), "stat": None},
        BF16,
        devices,
    )
    shared = share_stats(stat)
    behind = [along(after(inner[0], shared), "frame", 1), along(inner[1], "frame", 1)]
    plan = whole_plan(0) + shard_plan(1, "own") + shard_plan(2, "other")
    for k, step in enumerate((0, 3, 1, 2)):
        plan += ring_plan(3 + k, CUT, 9, "own", 1, step) + ring_plan(7 + k, CUT, 9, "other", 1, step)
    kernel_two = ([two, shard_two, swap_core(after(shard_two, base)), *held, *swapped], plan)
    norm_two = (shared, flags, place, row(gain_two), row(offset_two))

    hidden = lambda i, j: [0] + rows(1)(i, j)
    extras = {"bias": row(bias_two), "base": base}
    (late,) = block_conv(
        "conv_two_late",
        [behind[1], *inner],
        [(k, range(1), 0, RH + 2, rows(1) if k else hidden) for k in range(3)],
        [1],
        RH,
        [(1, a, a) for a in range(3)],
        *norm_two,
        kernel_two,
        extras,
        BF16,
        devices,
    )
    late_halo = along(late, "frame", 1)
    (early,) = block_conv(
        "conv_two_early",
        [*behind, after(inner[0], late)],
        [(k, range(1), 0, RH + 2, hidden if k < FT else rows(1)) for k in range(3)],
        [0],
        RH,
        [(0, a, a) for a in range(3)],
        *norm_two,
        kernel_two,
        extras,
        BF16,
        devices,
    )
    early_halo = along(early, "frame", 1)
    out = upsample(1, [late_halo, early, late], weight_time, row(bias_time), None)
    return upsample(0, [early_halo, late_halo, early], weight_time, row(bias_time), out)


def solution(mesh):
    placed = (
        P(None, ("frame", "height")),
        P("frame"),
        P(),
        P(),
        P(),
        P(),
        P(None, None, None, None, "height"),
        P(),
        P(),
        P(),
        P(None, None, None, None, "height"),
        P(),
        P(),
        P(),
    )
    return jax.shard_map(
        on_device,
        mesh=mesh,
        in_specs=placed,
        out_specs=P("frame", "height", None, None),
        check_vma=False,
    )
```

```python
import functools

import jax
import jax.numpy as jnp
from jax import lax
from jax.experimental import pallas as pl
from jax.experimental.pallas import tpu as pltpu
from jax.sharding import PartitionSpec as P

GROUPS = 32
ZC = 16
FT = 2
RH = 4
WD = 104
WP = 112
CH = 512
CELLS = FT * RH * WD
F32 = jnp.float32
BF16 = jnp.bfloat16
NT = (((1,), (1,)), ((), ()))
TN = (((0,), (0,)), ((), ()))
VMEM = pl.BlockSpec(memory_space=pltpu.VMEM)
SMEM = pl.BlockSpec(memory_space=pltpu.SMEM)
ANY = pl.BlockSpec(memory_space=pl.ANY)
EXACT = lax.Precision.HIGHEST
LIMIT = 44 * 2**20


def along(value, axis, steps):
    count = lax.axis_size(axis)
    leading, last = (max(0, -steps), min(count, count - steps))
    return lax.ppermute(value, axis, [(source, source + steps) for source in range(leading, last)])


def spread(rows, cols, lanes_first, shift):
    one = lax.broadcasted_iota(jnp.int32, (rows, cols), 0)
    two = lax.broadcasted_iota(jnp.int32, (rows, cols), 1)
    lane, channel = (one, two) if lanes_first else (two, one)
    return (lane == channel // (CH // GROUPS) + shift).astype(F32)


def local_stats(values, stat_ref):
    cells = values.shape[0]
    total = jnp.broadcast_to(jnp.sum(values, axis=0, keepdims=True), (8, CH))
    size = cells * (CH // GROUPS)
    mean = jnp.dot(total, spread(CH, 128, False, 0), precision=EXACT, preferred_element_type=F32) / size
    per_channel = jnp.dot(mean, spread(128, CH, True, 0), precision=EXACT, preferred_element_type=F32)
    centered = values - per_channel[:1]
    square = jnp.broadcast_to(jnp.sum(centered * centered, axis=0, keepdims=True), (8, CH))
    spread_sq = jnp.dot(square, spread(CH, 128, False, GROUPS), precision=EXACT, preferred_element_type=F32)
    stat_ref[...] = jnp.broadcast_to((mean + spread_sq)[:1], stat_ref.shape)


def combine_stats(stats_ref, size):
    stats = stats_ref[...]
    devices = stats.shape[0]
    group = lax.broadcasted_iota(jnp.int32, stats.shape, 1) < GROUPS
    means = jnp.where(group, stats, 0.0)
    mean = jnp.sum(means, axis=0, keepdims=True) / devices
    away = means - mean
    between = jnp.sum(away * away, axis=0, keepdims=True)
    within = pltpu.roll(jnp.broadcast_to(jnp.sum(stats, axis=0, keepdims=True), (8, 128)), 128 - GROUPS, 1)[:1]
    variance = jnp.where(group[:1], (within + size * between) / (size * devices), 0.0)
    inverse = lax.rsqrt(variance + 1e-06)
    both = jnp.concatenate([mean, inverse, jnp.zeros((6, 128), F32)], axis=0)
    both = jnp.dot(both, spread(128, CH, True, 0), precision=EXACT, preferred_element_type=F32)
    return both[:1], both[1:2]


def share_stats(stat):
    return lax.all_to_all(stat, ("frame", "height"), 0, 0, tiled=True)


def input_kernel(early_ref, behind_ref, own_ref, w_ref, bias_ref, base_ref, stat_ref):
    w = w_ref[...]
    lat = {}
    for k, ref in enumerate((early_ref, behind_ref, own_ref)):
        for i in range(FT):
            for r in range(RH + 6):
                value = ref[i, r].astype(F32)
                shifts = [value] + [pltpu.roll(value, 128 - e, 1) for e in (1, 2)]
                lat[k * FT + i, r] = jnp.concatenate([v.astype(BF16) for v in shifts], axis=0)
    for t in range(2 * FT):
        columns = []
        for r in range(RH + 4):
            columns.append(jnp.concatenate([lat[t + a, r + b] for a in range(3) for b in range(3)], axis=0))
        field = jnp.concatenate(columns, axis=1)
        total = lax.dot_general(field, w, TN, preferred_element_type=F32)
        total = (total + bias_ref[...]).astype(BF16).reshape(RH + 4, 128, CH)
        base_ref[t] = total[:, :WD]
    own = base_ref[FT:, 2 : RH + 2].reshape(CELLS, CH).astype(F32)
    local_stats(own, stat_ref)


def input_conv(latent, weight, bias, devices):
    return pl.pallas_call(
        input_kernel,
        in_specs=[VMEM] * 5,
        out_specs=[VMEM, VMEM],
        out_shape=[
            jax.ShapeDtypeStruct((2 * FT, RH + 4, WD, CH), BF16),
            jax.ShapeDtypeStruct((devices, 128), F32),
        ],
        compiler_params=pltpu.CompilerParams(vmem_limit_bytes=LIMIT),
        cost_estimate=pl.CostEstimate(flops=3 * 10**9, bytes_accessed=4 * 10**6, transcendentals=0),
        name="input_conv",
    )(*latent, weight, bias)


def after(value, earlier):
    return lax.optimization_barrier((value, earlier))[0]


CUT = 5


def quarter_kernel(w_ref, place_ref, out_ref, sems):
    copies = []
    for k in range(9 - CUT):
        rows = pl.multiple_of(place_ref[1] * 16, 16)
        source = w_ref.at[(CUT + k) % 3, :, (CUT + k) // 3, pl.ds(rows, 16)]
        copies.append(pltpu.make_async_copy(source, out_ref.at[k], sems.at[k]))
    for copy in copies:
        copy.start()
    for copy in copies:
        copy.wait()


def quarter_of(weight, place):
    return pl.pallas_call(
        quarter_kernel,
        in_specs=[ANY, SMEM],
        out_specs=VMEM,
        out_shape=jax.ShapeDtypeStruct((9 - CUT, 3, 16, CH), BF16),
        scratch_shapes=[pltpu.SemaphoreType.DMA((9 - CUT,))],
        cost_estimate=pl.CostEstimate(flops=0, bytes_accessed=10**6, transcendentals=0),
        name="take_quarter",
    )(weight, place)


def stack_kernel(*refs):
    *parts, out_ref, sems = refs
    copies = [pltpu.make_async_copy(part, out_ref.at[k], sems.at[k]) for k, part in enumerate(parts)]
    for copy in copies:
        copy.start()
    for copy in copies:
        copy.wait()


def stack(parts):
    return pl.pallas_call(
        stack_kernel,
        in_specs=[ANY] * len(parts),
        out_specs=VMEM,
        out_shape=jax.ShapeDtypeStruct((len(parts), *parts[0].shape), BF16),
        scratch_shapes=[pltpu.SemaphoreType.DMA((len(parts),))],
        compiler_params=pltpu.CompilerParams(vmem_limit_bytes=LIMIT),
        cost_estimate=pl.CostEstimate(flops=0, bytes_accessed=4 * 10**6, transcendentals=0),
        name="stack_parts",
    )(*parts)


def plane_groups():
    return [[(4 * y + x) * 8 + 2 * z + c for z in range(4) for x in range(4) for c in range(2)] for y in range(4)]


def plane_plan(array):
    return [
        (array, 8 * z + 2 * x + c, 0, 3, e, ("fixed", 2 * z + c, None, x))
        for e in range(3)
        for z in range(4)
        for x in range(4)
        for c in range(2)
    ]


def whole_plan(array):
    return [(array, k, k % 3, 1, k // 3, ("whole", 0, None, 0)) for k in range(CUT)]


def shard_plan(array, kind):
    return [(array, k // 3, k % 3, 1, k // 3, (kind, 0, None, 0)) for k in range(CUT, 9)]


Z_SHIFTS = (3, 1, 2)


def ring_plan(array, begin, end, kind, ring, step):
    plan = []
    k = begin
    while k < end:
        stop = min(end, k - k % 3 + 3)
        for i, z in enumerate(Z_SHIFTS):
            plan.append((array, (i, k - begin), k % 3, stop - k, k // 3, (kind, z, ring, step)))
        k = stop
    return plan


def conv_kernel(pieces, outs, height, products, taps, plan, weights, extras, *refs):
    refs = list(refs)
    raws = [refs.pop(0) for _ in pieces]
    stats_ref, flags_ref, place_ref, gain_ref, offset_ref = [refs.pop(0) for _ in range(5)]
    w_refs = [refs.pop(0) for _ in range(weights)]
    partial_ref = refs.pop(0) if "partial" in extras else None
    bias_ref = refs.pop(0) if "bias" in extras else None
    base_ref = refs.pop(0) if "base" in extras else None
    out_refs = [refs.pop(0) for _ in outs]
    stat_ref = refs.pop(0) if "stat" in extras else None
    field, wbuf, acc, sems = refs
    low, high = taps[0], taps[-1] + 1
    core, z = place_ref[0], place_ref[2]
    columns = sorted({copy[4] for copy in plan})
    copies = [[] for _ in columns]
    for array, index, tap, length, e, (kind, shift, ring, step) in plan:
        slot = columns.index(e)
        begin, end = max(tap, low), min(tap + length, high)
        if begin >= end:
            continue
        taps_of = pl.ds(begin - low, end - begin)
        if kind == "whole":
            source, target = w_refs[array].at[pl.ds(index, 1)], wbuf.at[slot, taps_of]
        else:
            block = 2 * lax.rem(z + shift, 4) + (1 - core if kind == "other" else core)
            rows, width = block * 64, 16
            if kind == "fixed":
                rows = 64 * shift + 16 * step
            elif ring is None:
                width = 64
            else:
                rows = rows + lax.rem(place_ref[ring] + step, 4) * 16
            if kind == "fixed":
                source = w_refs[array].at[index, pl.ds(begin, end - begin), :, e]
            elif ring is None:
                source = w_refs[array].at[pl.ds(begin, end - begin), :, index]
            else:
                source = w_refs[array].at[index[0], pl.ds(index[1] + begin - tap, end - begin)]
            target = wbuf.at[slot, taps_of, :, pl.ds(pl.multiple_of(rows, 16), width)]
        copies[slot].append(pltpu.make_async_copy(source, target, sems.at[slot]))
    for copy in copies[0]:
        copy.start()
    mean, inverse = combine_stats(stats_ref, CELLS * (CH // GROUPS))
    scale = inverse * gain_ref[...]
    offset = offset_ref[...]
    for raw, (frame, frames, row, rows, flag_of) in zip(raws, pieces):
        for i in frames:
            for j in range(rows):
                value = (raw[i, j].astype(F32) - mean) * scale + offset
                half = 0.5 * value
                value = half + half * jnp.tanh(half)
                for which in flag_of(i, j):
                    value = value * flags_ref[which]
                field[frame + i - frames[0], row + j, :WD] = value.astype(BF16)
                field[frame + i - frames[0], row + j, WD:] = jnp.zeros((WP - WD, CH), BF16)
    for later in copies[1:]:
        for copy in later:
            copy.start()
    total = jnp.zeros((len(outs) * height * WP, CH), F32)
    edge = jnp.zeros((1, CH), F32)
    for e, column in enumerate(columns):
        pltpu.make_async_copy(wbuf.at[e], wbuf.at[e], sems.at[e]).wait()
        for n, t in enumerate(outs):
            terms = [(f, a) for (out, f, a) in products if out == t]
            xs = [field[f, b : b + height].reshape(height * WP, CH) for f, a in terms for b in range(3)]
            ws = [wbuf[e, a - low, b] for f, a in terms for b in range(3)]
            acc[e, pl.ds(n * height * WP, height * WP)] = lax.dot_general(
                jnp.concatenate(xs, axis=1), jnp.concatenate(ws, axis=1), NT, preferred_element_type=F32
            )
    for e, column in enumerate(columns):
        if column == 0:
            total = total + jnp.concatenate([edge, acc[e, :-1]], axis=0)
        elif column == 1:
            total = total + acc[e]
        else:
            total = total + jnp.concatenate([acc[e, 1:], edge], axis=0)
    total = total.reshape(len(outs), height, WP, CH)[:, :, :WD]
    span = pl.ds(outs[0], len(outs))
    if partial_ref is not None:
        total = total + partial_ref[span]
    if bias_ref is not None:
        total = total + bias_ref[...]
    if base_ref is not None:
        total = total + base_ref[pl.ds(FT + outs[0], len(outs)), 2 : RH + 2].astype(F32)
    for n, out_ref in enumerate(out_refs):
        out_ref[...] = total[n : n + 1].astype(out_ref.dtype)
    if stat_ref is not None:
        own = total[:, 1 : RH + 1].astype(BF16).astype(F32)
        local_stats(own.reshape(CELLS, CH), stat_ref)


def block_conv(name, raws, pieces, outs, height, products, stats, flags, place, gain, offset, weight, extras, kind, devices):
    arrays, plan = weight
    columns = len({copy[4] for copy in plan})
    taps = sorted({a for _, _, a in products})
    frames = max(f for _, f, _ in products) + 1
    args = [*raws, stats, flags, place, gain, offset, *arrays]
    args += [extras[k] for k in ("partial", "bias", "base") if k in extras]
    specs = [*[VMEM] * len(raws), VMEM, SMEM, SMEM, VMEM, VMEM, *[ANY] * len(arrays)]
    specs += [VMEM] * (len(args) - len(specs))
    shapes = [jax.ShapeDtypeStruct((1, height, WD, CH), kind)] * len(outs)
    if "stat" in extras:
        shapes.append(jax.ShapeDtypeStruct((devices, 128), F32))
    return pl.pallas_call(
        functools.partial(conv_kernel, pieces, outs, height, products, taps, plan, len(arrays), tuple(extras)),
        in_specs=specs,
        out_specs=[VMEM] * len(shapes),
        out_shape=shapes,
        scratch_shapes=[
            pltpu.VMEM((frames, height + 2, WP, CH), BF16),
            pltpu.VMEM((columns, len(taps), 3, CH, CH), BF16),
            pltpu.VMEM((columns, len(outs) * height * WP, CH), F32),
            pltpu.SemaphoreType.DMA((columns,)),
        ],
        compiler_params=pltpu.CompilerParams(vmem_limit_bytes=LIMIT if "stat" in extras else 60 * 2**20),
        cost_estimate=pl.CostEstimate(
            flops=len(products) * 2 * 3 * columns * height * WP * CH * CH, bytes_accessed=16 * 10**6, transcendentals=0
        ),
        name=name,
    )(*args)


def upsample_kernel(*refs):
    first, second, third, w_ref, bias_ref = refs[:5]
    out_ref, field = refs[-2:]

    @pl.when(pl.program_id(0) == 0)
    def _():
        for k, ref in enumerate((first, second, third)):
            for r in range(RH):
                field[k, r, :WD] = ref[0, r]
                field[k, r, WD:] = jnp.zeros((WP - WD, CH), BF16)

    parts = jnp.concatenate([field[k].reshape(RH * WP, CH) for k in range(3)], axis=1)
    total = jnp.dot(parts, w_ref[...].reshape(3 * CH, CH // 2), preferred_element_type=F32) + bias_ref[...]
    total = total.astype(BF16).reshape(RH, WP, CH // 2)
    twice = lax.broadcasted_iota(jnp.int32, (2 * WD, WP), 0) // 2 == lax.broadcasted_iota(jnp.int32, (2 * WD, WP), 1)
    twice = twice.astype(F32).astype(BF16)
    for r in range(RH):
        wide = jnp.dot(twice, total[r], preferred_element_type=F32).astype(BF16)
        out_ref[0, 2 * r] = wide
        out_ref[0, 2 * r + 1] = wide


def upsample(t, frames, weight, bias, out):
    frame = pl.BlockSpec((1, RH, WD, CH), lambda s: (0, 0, 0, 0))
    return pl.pallas_call(
        upsample_kernel,
        grid=(4,),
        in_specs=[
            frame,
            frame,
            frame,
            pl.BlockSpec((3, CH, CH // 2), lambda s: (0, 0, s)),
            pl.BlockSpec((1, CH // 2), lambda s: (0, s)),
            *([] if out is None else [ANY]),
        ],
        out_specs=pl.BlockSpec((1, 2 * RH, 2 * WD, CH // 2), lambda s: (2 * t + s // 2, 0, 0, s % 2)),
        out_shape=jax.ShapeDtypeStruct((2 * FT, 2 * RH, 2 * WD, CH), BF16),
        scratch_shapes=[pltpu.VMEM((3, RH, WP, CH), BF16)],
        input_output_aliases={} if out is None else {5: 0},
        compiler_params=pltpu.CompilerParams(vmem_limit_bytes=LIMIT),
        cost_estimate=pl.CostEstimate(flops=15 * 10**8, bytes_accessed=6 * 10**6, transcendentals=0),
        name="upsample",
    )(*frames, weight, bias, *([] if out is None else [out]))


def deal_kernel(tokens_ref, line_ref, column_ref, tile_ref, tile_down_ref, out_ref):
    tiles = out_ref.shape[0]
    count = tokens_ref.shape[1]
    tile = tile_ref[...]
    same = tile_down_ref[...] == tile
    earlier = lax.broadcasted_iota(jnp.int32, (count, count), 0) < lax.broadcasted_iota(jnp.int32, (count, count), 1)
    rank = jnp.sum((same & earlier).astype(F32), axis=0, keepdims=True)
    slot = tile * 128 + rank.astype(jnp.int32)
    onto = lax.broadcasted_iota(jnp.int32, (tiles * 128, count), 0) == slot
    rest = jnp.zeros((14, count), F32)
    value = [tokens_ref[...].astype(F32), line_ref[...].astype(F32), column_ref[...].astype(F32), rest]
    value = jnp.concatenate(value, axis=0).astype(BF16)
    dealt = lax.dot_general(value, onto.astype(F32).astype(BF16), NT, preferred_element_type=F32).astype(BF16)
    for g in range(tiles):
        for k in range(3):
            near = g + k - 1
            if 0 <= near < tiles:
                out_ref[g, k] = dealt[:, near * 128 : near * 128 + 128]
            else:
                out_ref[g, k] = jnp.zeros((32, 128), BF16)


def place_kernel(dealt_ref, first_ref, out_ref):
    blocks = [dealt_ref[i, k].astype(F32) for i in range(dealt_ref.shape[0]) for k in range(3)]
    dealt = jnp.concatenate(blocks, axis=1)
    value, line, column = dealt[:ZC], dealt[ZC : ZC + 1], dealt[ZC + 1 : ZC + 2]
    count = dealt.shape[1]
    first = first_ref[0]
    field = []
    for t in range(FT):
        for i in range(RH + 6):
            row = first + i
            wanted = jnp.where((row >= 0) & (row < 32), t * 32 + row, -1).astype(F32)
            field.append(jnp.where(line == wanted, value, 0.0))
    onto = lax.broadcasted_iota(jnp.int32, (128, count), 0).astype(F32) == column
    placed = lax.dot_general(
        jnp.concatenate(field, axis=0).astype(BF16), onto.astype(F32).astype(BF16), NT, preferred_element_type=F32
    )
    out_ref[...] = placed.astype(BF16).reshape(out_ref.shape)


def latent_own(tokens, token_pos):
    tiles = lax.axis_size("height")
    mine = lax.axis_index("height")
    count = tokens.shape[1]
    places = lax.dynamic_slice_in_dim(token_pos, mine * count, count, 0)
    line = places // WD - lax.axis_index("frame") * (FT * RH * tiles)
    column = places % WD + 1
    tile = line % (RH * tiles) // RH
    params = pltpu.CompilerParams(vmem_limit_bytes=LIMIT)
    cost = pl.CostEstimate(flops=3 * 10**8, bytes_accessed=10**6, transcendentals=0)
    across = lambda v: v.reshape(1, count)
    dealt = pl.pallas_call(
        deal_kernel,
        in_specs=[VMEM] * 5,
        out_specs=VMEM,
        out_shape=jax.ShapeDtypeStruct((tiles, 3, 32, 128), BF16),
        compiler_params=params,
        cost_estimate=cost,
        name="deal_tokens",
    )(tokens, across(line), across(column), across(tile), tile.reshape(count, 1))
    dealt = lax.all_to_all(dealt, "height", 0, 0, tiled=True)
    return pl.pallas_call(
        place_kernel,
        in_specs=[VMEM, SMEM],
        out_specs=VMEM,
        out_shape=jax.ShapeDtypeStruct((FT, RH + 6, ZC, 128), BF16),
        compiler_params=params,
        cost_estimate=cost,
        name="place_tokens",
    )(dealt, (mine * RH - 3).reshape(1).astype(jnp.int32))


def latent_slabs(own):
    return along(own, "frame", 2), along(own, "frame", 1), own


def on_device(
    tokens,
    token_pos,
    weight_in,
    bias_in,
    gain_one,
    offset_one,
    weight_one,
    bias_one,
    gain_two,
    offset_two,
    weight_two,
    bias_two,
    weight_time,
    bias_time,
):
    devices = lax.axis_size("frame") * lax.axis_size("height")
    slab, tile = lax.axis_index("frame"), lax.axis_index("height")
    place = jnp.stack([tile % 2, slab // 4, tile // 2, slab % 4]).astype(jnp.int32)
    flags = jnp.stack([slab > 0, tile > 0, tile < lax.axis_size("height") - 1]).astype(F32)
    row = lambda v: v.reshape(1, -1)

    def send_y(v, k):
        return lax.ppermute(v, "frame", [(4 * y + x, 4 * ((y + k) % 4) + x) for y in range(4) for x in range(4)])

    def swap_core(v):
        return lax.ppermute(v, "height", [(i, i ^ 1) for i in range(8)])

    def send_z(v, k):
        return lax.ppermute(v, "height", [(i, (i + 2 * k) % 8) for i in range(8)])

    shard_one, shard_two = jnp.swapaxes(weight_one, 3, 4), jnp.swapaxes(weight_two, 3, 4)
    quarter_one = lax.dynamic_slice(shard_one, (0, 0, 0, 16 * (slab % 4), 0), (3, 3, 3, 16, CH))
    quarter_two = quarter_of(after(shard_two, quarter_one), place)
    one = lax.all_gather(quarter_one, ("frame", "height"), axis_index_groups=plane_groups())
    sent = [send_z(quarter_two, k) for k in (1, 3, 2)]
    own = latent_own(after(tokens, quarter_one), token_pos)
    latent = latent_slabs(own)
    near = stack([after(v, latent[0]) for v in sent])
    held = [send_y(near, k) if k else near for k in (0, 1, -1, 2)]
    base, stat = input_conv([after(v, near) for v in latent], weight_in.reshape(-1, CH), row(bias_in), devices)
    shared = share_stats(stat)
    taps_two = jnp.transpose(after(shard_two, base), (2, 0, 1, 3, 4)).reshape(9, 3, -1, CH)[:CUT]
    two = lax.all_gather(taps_two, "height", axis=2, tiled=True)
    swapped = [swap_core(v) for v in held]

    def rows(beyond):
        return lambda i, j: [1] if j < beyond else [2] if j >= RH + beyond else []

    everything = lambda i, j: ([0] if i < FT else []) + rows(2)(i, j)
    norm_one = (shared, flags, place, row(gain_one), row(offset_one))
    common = ([after(base, tuple(held))], [(0, range(2 * FT), 0, RH + 4, everything)], [0, 1], RH + 2, [(t, t + a, a) for t in range(FT) for a in range(3)])
    *inner, stat = block_conv(
        "conv_one",
        *common,
        *norm_one,
        ([one], plane_plan(0)),
        {"bias": row(bias_one), "stat": None},
        BF16,
        devices,
    )
    shared = share_stats(stat)
    behind = [along(after(inner[0], shared), "frame", 1), along(inner[1], "frame", 1)]
    plan = whole_plan(0) + shard_plan(1, "own") + shard_plan(2, "other")
    for k, step in enumerate((0, 3, 1, 2)):
        plan += ring_plan(3 + k, CUT, 9, "own", 1, step) + ring_plan(7 + k, CUT, 9, "other", 1, step)
    kernel_two = ([two, shard_two, swap_core(after(shard_two, base)), *held, *swapped], plan)
    norm_two = (shared, flags, place, row(gain_two), row(offset_two))

    hidden = lambda i, j: [0] + rows(1)(i, j)
    extras = {"bias": row(bias_two), "base": base}
    (late,) = block_conv(
        "conv_two_late",
        [behind[1], *inner],
        [(k, range(1), 0, RH + 2, rows(1) if k else hidden) for k in range(3)],
        [1],
        RH,
        [(1, a, a) for a in range(3)],
        *norm_two,
        kernel_two,
        extras,
        BF16,
        devices,
    )
    late_halo = along(late, "frame", 1)
    (early,) = block_conv(
        "conv_two_early",
        [*behind, after(inner[0], late)],
        [(k, range(1), 0, RH + 2, hidden if k < FT else rows(1)) for k in range(3)],
        [0],
        RH,
        [(0, a, a) for a in range(3)],
        *norm_two,
        kernel_two,
        extras,
        BF16,
        devices,
    )
    early_halo = along(early, "frame", 1)
    out = upsample(1, [late_halo, early, late], weight_time, row(bias_time), None)
    return upsample(0, [early_halo, late_halo, early], weight_time, row(bias_time), out)


def solution(mesh):
    placed = (
        P(None, ("frame", "height")),
        P("frame"),
        P(),
        P(),
        P(),
        P(),
        P(None, None, None, None, "height"),
        P(),
        P(),
        P(),
        P(None, None, None, None, "height"),
        P(),
        P(),
        P(),
    )
    return jax.shard_map(
        on_device,
        mesh=mesh,
        in_specs=placed,
        out_specs=P("frame", "height", None, None),
        check_vma=False,
    )
```
